32 devices in a mesh: dp: 4 (over y, x), row: 4 (over z), col: 2 (over core).
Axes of the slice: x: 2, y: 2, z: 4, core: 2. Of those that a mesh axis runs over, the one named last changes fastest.
Arguments:
- tokens: bfloat16 [4096, 896], P(('dp', 'row')), may hold values from -6 to 6
- segment_ids: int32 [4096], P(('dp', 'row')), may hold values from 0 to 2, as said below
- attn_gain: bfloat16 [896], replicated, may hold values from 0.099609375 to 1.8984375
- w_query: bfloat16 [896, 896], P('row', 'col'), may hold values from -0.1875 to 0.1875
- b_query: bfloat16 [896], P('col'), may hold values from -3 to 3
- w_key: bfloat16 [896, 128], P('row', 'col'), may hold values from -0.1875 to 0.1875
- b_key: bfloat16 [128], P('col'), may hold values from -3 to 3
- w_value: bfloat16 [896, 128], P('row', 'col'), may hold values from -0.1875 to 0.1875
- b_value: bfloat16 [128], P('col'), may hold values from -0.59765625 to 0.59765625
- w_out: bfloat16 [896, 896], P('col', 'row'), may hold values from -1 to 1
- ffn_gain: bfloat16 [896], replicated, may hold values from 0.099609375 to 1.8984375
- w_gate: bfloat16 [896, 4864], P('row', 'col'), may hold values from -0.1875 to 0.1875
- w_up: bfloat16 [896, 4864], P('row', 'col'), may hold values from -0.1875 to 0.1875
- w_down: bfloat16 [4864, 896], P('col', 'row'), may hold values from -0.078125 to 0.078125
- out_grad: bfloat16 [4096, 896], P(('dp', 'row')), may hold values from -8 to 8
Outputs:
- output: bfloat16 [4096, 896], P(('dp', 'row'))
- grad_tokens: bfloat16 [4096, 896], P(('dp', 'row'))
- grad_attn_gain: float32 [896], replicated
- grad_w_query: float32 [896, 896], P('row', 'col')
- grad_b_query: float32 [896], P('col')
- grad_w_key: float32 [896, 128], P('row', 'col')
- grad_b_key: float32 [128], P('col')
- grad_w_value: float32 [896, 128], P('row', 'col')
- grad_b_value: float32 [128], P('col')
- grad_w_out: float32 [896, 896], P('col', 'row')
- grad_ffn_gain: float32 [896], replicated
- grad_w_gate: float32 [896, 4864], P('row', 'col')
- grad_w_up: float32 [896, 4864], P('row', 'col')
- grad_w_down: float32 [4864, 896], P('col', 'row')
The draws below stay inside these ranges and needn't reach their ends.
Inputs may be any that keep to these rules, and one draw needn't show every extreme that they name: `segment_ids`: within each sequence of 1024 tokens the ids never fall; id 1 is one document that begins among the first 256 tokens and ends among the last 256; id 0 covers the tokens before it and id 2 those after it.
All inputs are finite; a program needn't handle non-finite values.
Results may differ from the reference program's by a relative error of at most 0.035.
Values may be sent and summed in bfloat16 or wider, within the bound.
No kernel may reach another device: no remote copies, remote signals or barrier semaphores. Data moves between devices by JAX's collectives and lax.ppermute only.
A program may use at most 128 MiB of HBM per device.

```python
import jax
import jax.numpy as jnp
from jax import lax

D = 896
H = 14
KVH = 2
HD = 64
FF = 4864
LEN = 1024
ROW_TOK = 256
SEQS = 4
TOKENS = 4096


def draw_segment_ids(key, part):
    key = jax.random.fold_in(key, 11)
    begin_key, end_key = jax.random.split(key)
    begin_at = jax.random.randint(begin_key, (SEQS, 1), 1, ROW_TOK)
    end_at = jax.random.randint(end_key, (SEQS, 1), LEN - ROW_TOK + 1, LEN)
    position = jnp.arange(LEN, dtype=jnp.int32)[None, :]
    doc_ids = (position >= begin_at).astype(jnp.int32) + (position >= end_at).astype(jnp.int32)
    return doc_ids.reshape(TOKENS)


def strengthened(array, rng, source, target, shards_of, factor):
    owner, partner = [(jnp.arange(array.shape[axis_at]) // (array.shape[axis_at] // shards_of)).reshape([-1 if axis == axis_at else 1 for axis in range(array.ndim)]) for axis_at in (source, target)]
    chosen = jax.random.permutation(rng, shards_of)[partner]
    strong = (owner == chosen) | (owner == (partner + shards_of // 2) % shards_of)
    return jnp.where(strong, factor * array, array)


def shard_levels(own_key, dims, shards, low, largest):
    level = 1.0
    for axis_at, parts in shards:
        steps = jax.random.uniform(jax.random.fold_in(jax.random.fold_in(own_key, 6), axis_at), (parts,), jnp.float32, low / len(shards), largest / len(shards))
        level = level * jnp.repeat(jnp.exp(steps), dims[axis_at] // parts).reshape((-1,) + (1,) * (len(dims) - 1 - axis_at))
    return level


def bell_draw(own_key, shape, deviation, bound, cuts=(), held_as=jnp.bfloat16):
    array = jax.random.normal(own_key, shape, jnp.float32) * deviation
    if len(cuts) > 0:
        array = shard_levels(own_key, shape, cuts, -0.22, 0.18) * array
    return jnp.clip(array, min=-bound, max=bound).astype(held_as)


def gaussian_with(own_key, extent, width, reach, cuts, heavy, kind=jnp.bfloat16):
    values = width * jax.random.normal(own_key, extent, jnp.float32)
    if cuts:
        values = values * shard_levels(own_key, extent, cuts, -0.22, 0.18)
    return jnp.clip(strengthened(values, jax.random.fold_in(own_key, 3), *heavy), -reach, reach).astype(kind)


def setup_inputs(seed: int = 0) -> dict:
    keys = jax.random.split(jax.random.key(seed), 16)
    return {
        "tokens": bell_draw(keys[0], (TOKENS, D), 1.0, 6.0, ((0, 16),)),
        "segment_ids": draw_segment_ids(jax.random.fold_in(keys[15], 71), 0),
        "attn_gain": jnp.clip(1.0 + 0.18 * jax.random.normal(keys[2], (D,), jnp.float32), 0.099609375, 1.8984375).astype(jnp.bfloat16),
        "w_query": bell_draw(keys[3], (D, H * HD), D ** -0.5, 0.1875, ((0, 4), (1, 2))),
        "b_query": bell_draw(keys[4], (H * HD,), 0.5, 3.0, ((0, 2),)),
        "w_key": bell_draw(keys[5], (D, KVH * HD), D ** -0.5, 0.1875, ((0, 4), (1, 2))),
        "b_key": bell_draw(keys[6], (KVH * HD,), 0.5, 3.0, ((0, 2),)),
        "w_value": bell_draw(keys[7], (D, KVH * HD), D ** -0.5, 0.1875, ((0, 4), (1, 2))),
        "b_value": bell_draw(keys[8], (KVH * HD,), 0.1, 0.59765625, ((0, 2),)),
        "w_out": bell_draw(keys[9], (H * HD, D), (H * HD // 32) ** -0.5, 1.0, ((0, 2), (1, 4))),
        "ffn_gain": jnp.clip(1.0 + 0.18 * jax.random.normal(keys[10], (D,), jnp.float32), 0.099609375, 1.8984375).astype(jnp.bfloat16),
        "w_gate": bell_draw(keys[11], (D, FF), D ** -0.5, 0.1875, ((0, 4), (1, 2))),
        "w_up": bell_draw(keys[12], (D, FF), D ** -0.5, 0.1875, ((0, 4), (1, 2))),
        "w_down": bell_draw(keys[13], (FF, D), FF ** -0.5, 0.078125, ((0, 2), (1, 4))),
        "out_grad": gaussian_with(keys[14], (TOKENS, D), 1.0, 8.0, ((0, 16),), (0, 1, 16, 2.0)),
    }


NORM_EPS = 1e-06
ROPE_BASE = 1000000.0
NEG_BIG = -1e+30
PRECISE = lax.Precision.HIGHEST

@jax.custom_vjp
def low(v):
    return lax.optimization_barrier(v.astype(jnp.bfloat16)).astype(jnp.float32)

@jax.custom_vjp
def low_back(v):
    return v

def low_keep(v):
    return (low(v), None)

def low_pass(kept, grad):
    return (grad,)

def back_keep(v):
    return (v, None)

def back_low(kept, grad):
    return (low(grad),)
low.defvjp(low_keep, low_pass)
low_back.defvjp(back_keep, back_low)

def matmul(left, right):
    return jnp.dot(left, right, precision=PRECISE)

def norm_rows(values, gain):
    inv_rms = lax.rsqrt(lax.optimization_barrier(jnp.mean(values * values, axis=1, keepdims=True)) + NORM_EPS)
    return values * inv_rms * gain[None, :]

def rope_tables(positions, head_size):
    ladder = jnp.arange(head_size // 2, dtype=jnp.float32) * (2.0 / head_size)
    frequency = jnp.exp(-ladder * jnp.log(ROPE_BASE))
    angles = positions[:, None] * frequency[None, :]
    return (jnp.cos(angles), jnp.sin(angles))

def rotate(values, cos_table, sin_table):
    half_size = values.shape[-1] // 2
    lower = values[..., :half_size]
    upper = values[..., half_size:]
    cos_part = cos_table[:, None, :]
    sin_part = sin_table[:, None, :]
    return jnp.concatenate([lower * cos_part - upper * sin_part, upper * cos_part + lower * sin_part], axis=-1)

def attend_block(query_block, query_pos, query_seg, key_rows, value_rows, key_pos, key_seg):
    raw_scores = jnp.einsum('bkgd,nkd->kgbn', query_block, key_rows, precision=PRECISE) * HD ** (-0.5)
    scores = low_back(raw_scores)
    allowed = (key_pos[None, :] <= query_pos[:, None]) & (key_seg[None, :] == query_seg[:, None])
    masked = jnp.where(allowed, scores, NEG_BIG)
    row_top = lax.optimization_barrier(jnp.max(masked, axis=-1, keepdims=True))
    weights = jnp.exp(masked - row_top)
    probs_low = low(weights / lax.optimization_barrier(jnp.sum(weights, axis=-1, keepdims=True)))
    return jnp.einsum('kgbn,nkd->bkgd', probs_low, value_rows, precision=PRECISE)

def forward_sequence(weights_in, values_in, seg_row):
    attn_gain, w_query, b_query, w_key, b_key, w_value, b_value, w_out, ffn_gain, w_gate, w_up, w_down = weights_in
    length = values_in.shape[0]
    group_size = H // KVH
    normed1 = low(norm_rows(values_in, attn_gain))
    tok_pos = jnp.arange(length, dtype=jnp.int32)
    cos_table, sin_table = rope_tables(tok_pos.astype(jnp.float32), HD)
    query_lin = low_back(matmul(normed1, w_query) + b_query[None, :])
    key_lin = low_back(matmul(normed1, w_key) + b_key[None, :])
    value_rows = low(low_back(matmul(normed1, w_value) + b_value[None, :])).reshape(length, KVH, HD)
    query_rot = low(rotate(query_lin.reshape(length, H, HD), cos_table, sin_table))
    key_rot = low(rotate(key_lin.reshape(length, KVH, HD), cos_table, sin_table))
    block_rows = min(512, length)
    block_count = length // block_rows
    query_blocks = query_rot.reshape(block_count, block_rows, KVH, group_size, HD)

    def one_block(block_items):
        query_block, query_pos, query_seg = block_items
        return attend_block(query_block, query_pos, query_seg, key_rot, value_rows, tok_pos, seg_row)
    heads_out = lax.map(jax.checkpoint(one_block), (query_blocks, tok_pos.reshape(block_count, block_rows), seg_row.reshape(block_count, block_rows)))
    attn_heads = low(low_back(heads_out.reshape(length, H * HD)))
    residual = values_in + low_back(matmul(attn_heads, w_out))
    normed2 = low(norm_rows(residual, ffn_gain))
    gate_lin = low_back(matmul(normed2, w_gate))
    up_lin = low_back(matmul(normed2, w_up))
    hidden = low(jax.nn.silu(gate_lin) * up_lin)
    return residual + low_back(matmul(hidden, w_down))

def reference(tokens, segment_ids, attn_gain, w_query, b_query, w_key, b_key, w_value, b_value, w_out, ffn_gain, w_gate, w_up, w_down, out_grad):
    weights_all = (attn_gain.astype(jnp.float32), w_query.astype(jnp.float32), b_query.astype(jnp.float32), w_key.astype(jnp.float32), b_key.astype(jnp.float32), w_value.astype(jnp.float32), b_value.astype(jnp.float32), w_out.astype(jnp.float32), ffn_gain.astype(jnp.float32), w_gate.astype(jnp.float32), w_up.astype(jnp.float32), w_down.astype(jnp.float32))
    inputs = tokens.astype(jnp.float32).reshape(SEQS, LEN, D)
    seg_all = segment_ids.reshape(SEQS, LEN)
    cotangent = out_grad.astype(jnp.float32).reshape(SEQS, LEN, D)
    zero_grads = jax.tree.map(jnp.zeros_like, weights_all)

    def one_sequence(totals, seq_items):
        values_in, seg_row, grad_row = seq_items

        def run_layer(weights_in, values_here):
            return forward_sequence(weights_in, values_here, seg_row)
        result, pullback = jax.vjp(run_layer, weights_all, values_in)
        grad_weights, grad_values = pullback(grad_row)
        totals = jax.tree.map(jnp.add, totals, grad_weights)
        return (totals, (result.astype(jnp.bfloat16), grad_values.astype(jnp.bfloat16)))
    totals, (outputs, grad_inputs) = lax.scan(one_sequence, zero_grads, (inputs, seg_all, cotangent))
    return (outputs.reshape(TOKENS, D), grad_inputs.reshape(TOKENS, D), totals[0], totals[1], totals[2], totals[3], totals[4], totals[5], totals[6], totals[7], totals[8], totals[9], totals[10], totals[11])
```

```python
import functools

import jax
import jax.numpy as jnp
from jax import lax
from jax.experimental import pallas as pl
from jax.experimental.pallas import tpu as pltpu
from jax.sharding import PartitionSpec as P

HD = 64
HALF = HD // 2
NORM_EPS = 1e-06
ROPE_BASE = 1000000.0
NEG_BIG = -1e30
LANES = 128
EXTRA_ROWS = 16
BF16 = jnp.bfloat16
F32 = jnp.float32


def dot_rows(left, right):
    return lax.dot_general(left, right, (((0,), (0,)), ((), ())), preferred_element_type=F32)


def dot_cols(left, right):
    return lax.dot_general(left, right, (((1,), (1,)), ((), ())), preferred_element_type=F32)


def dot(left, right):
    return jnp.dot(left, right, preferred_element_type=F32)


def inverse_rms(values):
    return lax.rsqrt(jnp.mean(values * values, axis=1, keepdims=True) + NORM_EPS)


def norm_back(gradient, unit_rows, inv_rms, gain):
    scaled = gradient * gain
    inner = jnp.mean(scaled * unit_rows, axis=1, keepdims=True)
    return (inv_rms * (scaled - unit_rows * inner), jnp.sum(gradient * unit_rows, axis=0))


def swap_core(value):
    return lax.ppermute(value, "col", [(0, 1), (1, 0)])


def dp_step(value, step):
    pairs = []
    for group in range(4):
        for core in range(2):
            bit = 1 << ((step + core) % 2)
            pairs.append((group * 2 + core, (group ^ bit) * 2 + core))
    return lax.ppermute(value, ("dp", "col"), pairs)


def dp_gather(value):
    first = dp_step(value, 0)
    pair = jnp.stack([value, first])
    second = dp_step(pair, 1)
    return jnp.concatenate([pair, second], axis=0)


def dp_scatter_sum(parts):
    first = dp_step(parts[2:].astype(BF16), 1)
    pair = parts[:2] + first.astype(F32)
    second = dp_step(pair[1].astype(BF16), 0)
    return pair[0] + second.astype(F32)


def dp_scatter_sum_cols(parts):
    kept = parts[0::2].astype(F32)
    pair = kept + dp_step(parts[1::2], 0).astype(F32)
    return pair[0] + dp_step(pair[1].astype(BF16), 1).astype(F32)


def dp_exchange(parts):
    first = dp_step(parts[1::2], 0)
    kept = jnp.stack([parts[0], first[0]])
    onward = jnp.stack([parts[2], first[1]])
    return jnp.concatenate([kept, dp_step(onward, 1)], axis=0)


def dp_slots(group, core):
    slots = []
    for j in range(4):
        relative = group ^ j
        flipped = (relative & 1) * 2 + (relative >> 1)
        slots.append(jnp.where(core == 0, relative, flipped))
    return slots


def pick(stacked, place, axis=0):
    return lax.dynamic_index_in_dim(stacked, place, axis=axis, keepdims=False)


def half_turn(values):
    lane = lax.broadcasted_iota(jnp.int32, values.shape, 1) % HD
    return jnp.where(lane < HALF, -jnp.roll(values, -HALF, axis=1), jnp.roll(values, HALF, axis=1))


def mask_bias(q_meta, k_meta):
    allowed = (k_meta[0:1, :] <= q_meta[:, 0:1]) & (k_meta[1:2, :] == q_meta[:, 1:2])
    return jnp.where(allowed, 0.0, NEG_BIG)


def attend_kernel(heads, q_ref, kv_ref, qm_ref, km_ref, out_ref, lse_ref, bias_ref):
    bias_ref[...] = mask_bias(qm_ref[...], km_ref[...])
    keys = kv_ref[:, :HD]
    values = kv_ref[:, HD:]
    lane = lax.broadcasted_iota(jnp.int32, lse_ref.shape, 1)
    lse_all = jnp.zeros(lse_ref.shape, F32)
    outs = []
    for head in range(heads):
        cols = slice(head * HD, (head + 1) * HD)
        scores = dot_cols(q_ref[:, cols], keys) + bias_ref[...]
        top = jnp.max(scores, axis=1, keepdims=True)
        weights = jnp.exp(scores - top)
        total = jnp.sum(weights, axis=1, keepdims=True)
        outs.append(dot(weights.astype(BF16), values) / total)
        lse_all = jnp.where(lane == head, top + jnp.log(total), lse_all)
    out_ref[...] = jnp.concatenate(outs, axis=1)
    lse_ref[...] = lse_all


def attend_back_kernel(
    heads, q_ref, kv_ref, qm_ref, km_ref, out_ref, lse_ref, do_ref, dq_ref, dkv_ref, bias_ref
):
    bias_ref[...] = mask_bias(qm_ref[...], km_ref[...])
    keys = kv_ref[:, :HD]
    values = kv_ref[:, HD:]
    d_keys = jnp.zeros((kv_ref.shape[0], HD), F32)
    d_values = jnp.zeros((kv_ref.shape[0], HD), F32)
    dqs = []
    for head in range(heads):
        cols = slice(head * HD, (head + 1) * HD)
        queries = q_ref[:, cols]
        grads = do_ref[:, cols]
        delta = jnp.sum(grads.astype(F32) * out_ref[:, cols], axis=1, keepdims=True)
        scores = dot_cols(queries, keys) + bias_ref[...]
        probs = jnp.exp(scores - lse_ref[:, head : head + 1])
        d_probs = dot_cols(grads, values)
        d_scores = (probs * (d_probs - delta)).astype(BF16)
        dqs.append(dot(d_scores, keys) * HD ** (-0.5))
        d_keys = d_keys + dot_rows(d_scores, queries)
        d_values = d_values + dot_rows(probs.astype(BF16), grads)
    dq_ref[...] = jnp.concatenate(dqs, axis=1)
    dkv_ref[...] = jnp.concatenate([d_keys, d_values], axis=1)


def per_device(
    rows,
    tokens,
    segment_ids,
    attn_gain,
    w_query,
    b_query,
    w_key,
    b_key,
    w_value,
    b_value,
    w_out,
    ffn_gain,
    w_gate,
    w_up,
    w_down,
    out_grad,
):
    count, width = tokens.shape
    half = count // 2
    d_rows = w_query.shape[0]
    q_width = w_query.shape[1]
    qk_width = q_width + HD
    lin_width = qk_width + HD
    heads = q_width // HD
    units = w_gate.shape[1] // 4
    row = lax.axis_index("row")
    group = lax.axis_index("dp")
    core = lax.axis_index("col")
    slots = dp_slots(group, core)
    first_bit = jnp.where(core == 0, 1, 2)
    second_bit = 3 - first_bit
    targets = [group, group ^ first_bit, group ^ second_bit, group ^ 3]

    def shift(step):
        return [(i, (i + step) % rows) for i in range(rows)]

    def upward(step):
        return [(i, i + step) for i in range(rows - step)]

    def downward(step):
        return [(i + step, i) for i in range(rows - step)]

    w_lin = lax.all_gather(
        jnp.concatenate([w_query, w_key, w_value], axis=1), "row", axis=0, tiled=True
    )
    w_out_t = lax.all_gather(w_out.T, "row", axis=0, tiled=True)
    own_ffn = jnp.stack(
        [
            lax.dynamic_slice_in_dim(w_gate, group * units, units, axis=1),
            lax.dynamic_slice_in_dim(w_up, group * units, units, axis=1),
            lax.dynamic_slice_in_dim(w_down, group * units, units, axis=0).T,
        ]
    )
    ffn = jnp.zeros((3, rows, d_rows, units), BF16)
    for step in range(rows):
        piece = own_ffn if step == 0 else lax.ppermute(own_ffn, "row", shift(step))
        place = (row + rows - step) % rows
        ffn = lax.dynamic_update_slice(ffn, piece[:, None], (0, place, 0, 0))
    ffn = ffn.reshape(3, width, units)
    gate_w, up_w, down_t = ffn[0], ffn[1], ffn[2]

    def split_gather(values):
        own = dp_gather(lax.dynamic_slice_in_dim(values, core * half, half, axis=0))
        own = own.reshape(4 * half, width)
        return jnp.concatenate([own, swap_core(own)], axis=0)

    def split_scatter_sum(partial):
        parts = partial.reshape(2, 4, half, width)
        kept = parts[0] + swap_core(parts[1].astype(BF16)).astype(F32)
        own = dp_scatter_sum(kept).astype(BF16)
        other = swap_core(own)
        low = jnp.where(core == 0, own, other)
        high = jnp.where(core == 0, other, own)
        return jnp.concatenate([low, high], axis=0).astype(F32)

    inputs = tokens.astype(F32)
    gain_one = attn_gain.astype(F32)[None, :]
    gain_two = ffn_gain.astype(F32)[None, :]
    inv_one = inverse_rms(inputs)
    unit_one = inputs * inv_one
    normed1 = (unit_one * gain_one).astype(BF16)
    grad_all = split_gather(out_grad)
    normed1_all = dp_gather(normed1).reshape(4 * count, width)
    bias = jnp.concatenate([b_query, b_key, b_value]).astype(F32)[None, :]
    lin = dot(normed1, w_lin) + bias
    positions = row * count + jnp.arange(count, dtype=jnp.int32)
    ladder = (jnp.arange(HD, dtype=jnp.int32) % HALF).astype(F32) * (2.0 / HD)
    angles = positions.astype(F32)[:, None] * jnp.exp(-ladder * jnp.log(ROPE_BASE))[None, :]
    cos_one, sin_one = jnp.cos(angles), jnp.sin(angles)
    cos_table = jnp.tile(cos_one, (1, heads + 1))
    sin_table = jnp.tile(sin_one, (1, heads + 1))
    qk_lin = lin[:, :qk_width]
    qk_rot = qk_lin * cos_table + half_turn(qk_lin) * sin_table
    queries = (qk_rot[:, :q_width].astype(BF16).astype(F32) * HD ** (-0.5)).astype(BF16)
    kv_own = jnp.concatenate([qk_rot[:, q_width:], lin[:, qk_width:]], axis=1).astype(BF16)
    seg_rows = count // LANES
    seg_own = jnp.zeros((EXTRA_ROWS, LANES), BF16)
    seg_own = seg_own.at[:seg_rows].set(segment_ids.astype(BF16).reshape(seg_rows, LANES))
    kv_send = jnp.concatenate([kv_own, seg_own], axis=0)
    pieces = [kv_send] + [lax.ppermute(kv_send, "row", upward(step)) for step in range(1, rows)]
    kv_all = jnp.concatenate([piece[:count] for piece in pieces], axis=0)
    key_seg = jnp.concatenate(
        [piece[count : count + seg_rows].reshape(count) for piece in pieces]
    ).astype(jnp.int32)
    block = jnp.repeat(jnp.arange(rows, dtype=jnp.int32), count)
    within = jnp.tile(jnp.arange(count, dtype=jnp.int32), rows)
    key_pos = jnp.where(block <= row, (row - block) * count + within, 2**30)
    key_meta = jnp.zeros((8, rows * count), jnp.int32).at[0].set(key_pos).at[1].set(key_seg)
    query_meta = jnp.stack([positions, segment_ids], axis=1)
    key_count = rows * count
    attend_cost = 2 * heads * count * key_count * HD
    attn_out, log_sum = pl.pallas_call(
        functools.partial(attend_kernel, heads),
        out_shape=(
            jax.ShapeDtypeStruct((count, q_width), F32),
            jax.ShapeDtypeStruct((count, LANES), F32),
        ),
        scratch_shapes=[pltpu.VMEM((count, key_count), F32)],
        compiler_params=pltpu.CompilerParams(vmem_limit_bytes=40 * 2**20),
        cost_estimate=pl.CostEstimate(
            flops=2 * attend_cost,
            bytes_accessed=2**21,
            transcendentals=heads * count * key_count,
        ),
    )(queries, kv_all, query_meta, key_meta)
    attn_heads = attn_out.astype(BF16)
    branch = dot_cols(attn_heads, w_out_t).astype(BF16)
    residual = inputs + (branch.astype(F32) + swap_core(branch).astype(F32))

    inv_two = inverse_rms(residual)
    unit_two = residual * inv_two
    normed2 = (unit_two * gain_two).astype(BF16)
    normed2_all = split_gather(normed2)
    gate_lin = dot(normed2_all, gate_w)
    up_lin = dot(normed2_all, up_w)
    d_hidden = dot(grad_all, down_t)
    sigmoid_gate = jax.nn.sigmoid(gate_lin)
    silu_gate = gate_lin * sigmoid_gate
    hidden = (silu_gate * up_lin).astype(BF16)
    d_gate = (d_hidden * up_lin * sigmoid_gate * (1.0 + gate_lin * (1.0 - sigmoid_gate))).astype(
        BF16
    )
    d_up = (d_hidden * silu_gate).astype(BF16)
    d_normed2 = split_scatter_sum(dot_cols(d_gate, gate_w) + dot_cols(d_up, up_w))
    ffn_branch = split_scatter_sum(dot_cols(hidden, down_t))
    output = (residual + ffn_branch).astype(BF16)
    ffn_grads = jnp.stack(
        [
            dot_rows(normed2_all, d_gate).astype(BF16),
            dot_rows(normed2_all, d_up).astype(BF16),
            dot_rows(grad_all, hidden).astype(BF16),
        ]
    ).reshape(3, rows, d_rows, units)

    def row_scatter(parts, axis):
        own = pick(parts, row, axis)
        others = [
            lax.ppermute(pick(parts, (row + step) % rows, axis), "row", shift(step))
            for step in range(1, rows)
        ]
        return [own] + others

    def total(parts):
        summed = parts[0].astype(F32)
        for part in parts[1:]:
            summed = summed + part.astype(F32)
        return summed

    ffn_done = dp_gather(total(row_scatter(ffn_grads, 1)).astype(BF16))

    d_res_norm, grad_gain_two = norm_back(d_normed2, unit_two, inv_two, gain_two)
    d_residual = out_grad.astype(F32) + d_res_norm
    d_residual_low = d_residual.astype(BF16)
    d_heads = dot(d_residual_low, w_out_t).astype(BF16)
    out_cols = q_width // 4
    out_part = dot_rows(d_residual_low, attn_heads).astype(BF16).reshape(width, 4, out_cols)
    out_part = jnp.stack([pick(out_part, target, 1) for target in targets])
    out_sum = dp_scatter_sum_cols(out_part)
    dq_rot, dkv_all = pl.pallas_call(
        functools.partial(attend_back_kernel, heads),
        out_shape=(
            jax.ShapeDtypeStruct((count, q_width), F32),
            jax.ShapeDtypeStruct((key_count, 2 * HD), F32),
        ),
        scratch_shapes=[pltpu.VMEM((count, key_count), F32)],
        compiler_params=pltpu.CompilerParams(vmem_limit_bytes=48 * 2**20),
        cost_estimate=pl.CostEstimate(
            flops=5 * attend_cost,
            bytes_accessed=2**22,
            transcendentals=heads * count * key_count,
        ),
    )(queries, kv_all, query_meta, key_meta, attn_out, log_sum, d_heads)
    dkv_parts = dkv_all.astype(BF16).reshape(rows, count, 2 * HD)
    dkv = total(
        [dkv_parts[0]]
        + [lax.ppermute(dkv_parts[step], "row", downward(step)) for step in range(1, rows)]
    )
    dqk_rot = jnp.concatenate([dq_rot, dkv[:, :HD]], axis=1)
    dqk = dqk_rot * cos_table - half_turn(dqk_rot) * sin_table
    d_lin = jnp.concatenate([dqk, dkv[:, HD:]], axis=1).astype(BF16)
    d_normed1 = dot_cols(d_lin, w_lin).astype(BF16)
    d_normed1 = d_normed1.astype(F32) + swap_core(d_normed1).astype(F32)
    d_in_norm, grad_gain_one = norm_back(d_normed1, unit_one, inv_one, gain_one)
    grad_tokens = (d_residual + d_in_norm).astype(BF16)

    lin_cols = lin_width // 4
    d_lin_parts = d_lin.reshape(count, 4, lin_cols)
    d_lin_parts = jnp.stack([pick(d_lin_parts, target, 1) for target in targets])
    d_lin_all = dp_exchange(d_lin_parts).reshape(4 * count, lin_cols)
    lin_sum = dot_rows(normed1_all, d_lin_all)
    bias_sum = jnp.sum(d_lin_all.astype(F32), axis=0)
    pack_width = out_cols + lin_cols
    small = jnp.concatenate([grad_gain_one, grad_gain_two, bias_sum])
    small = jnp.pad(small, (0, EXTRA_ROWS // 2 * pack_width - small.shape[0]))

    def two_halves(values):
        high = values.astype(BF16)
        low = (values - high.astype(F32)).astype(BF16)
        return jnp.concatenate([high, low]).reshape(EXTRA_ROWS, pack_width)

    small_low = two_halves(small)
    attn_grads = jnp.concatenate([out_sum, lin_sum], axis=1).astype(BF16)
    attn_grads = attn_grads.reshape(rows, d_rows, pack_width)
    attn_grads = jnp.concatenate(
        [attn_grads, jnp.broadcast_to(small_low, (rows, EXTRA_ROWS, pack_width))], axis=1
    )
    received = row_scatter(attn_grads, 0)
    attn_sum = total([piece[:d_rows] for piece in received]).astype(BF16)
    small_parts = jnp.stack([piece[d_rows:] for piece in received])
    small_sum = jnp.zeros((EXTRA_ROWS, pack_width), F32)
    for place in range(rows):
        small_sum = small_sum + pick(small_parts, (row + rows - place) % rows).astype(F32)
    small_sum = small_sum[: EXTRA_ROWS // 2] + small_sum[EXTRA_ROWS // 2 :]
    attn_done = dp_gather(jnp.concatenate([attn_sum, two_halves(small_sum.reshape(-1))], axis=0))

    ffn_pieces = [pick(ffn_done, slot) for slot in slots]
    attn_pieces = [pick(attn_done, slot) for slot in slots]

    def joined(parts):
        return jnp.concatenate(parts, axis=1).astype(F32)

    grad_w_gate = joined([piece[0] for piece in ffn_pieces])
    grad_w_up = joined([piece[1] for piece in ffn_pieces])
    grad_w_down = joined([piece[2] for piece in ffn_pieces]).T
    grad_w_out = joined([piece[:d_rows, :out_cols] for piece in attn_pieces]).T
    grad_w_lin = joined([piece[:d_rows, out_cols:] for piece in attn_pieces])
    smalls = [
        piece[d_rows : d_rows + EXTRA_ROWS // 2].astype(F32).reshape(-1)
        + piece[d_rows + EXTRA_ROWS // 2 :].astype(F32).reshape(-1)
        for piece in attn_pieces
    ]
    gains = total([small_piece[: 2 * width] for small_piece in smalls])
    biases = jnp.concatenate(
        [small_piece[2 * width : 2 * width + lin_cols] for small_piece in smalls]
    )
    return (
        output,
        grad_tokens,
        gains[:width],
        grad_w_lin[:, :q_width],
        biases[:q_width],
        grad_w_lin[:, q_width:qk_width],
        biases[q_width:qk_width],
        grad_w_lin[:, qk_width:],
        biases[qk_width:],
        grad_w_out,
        gains[width:],
        grad_w_gate,
        grad_w_up,
        grad_w_down,
    )


def solution(mesh):
    return jax.shard_map(
        functools.partial(per_device, mesh.shape["row"]),
        mesh=mesh,
        in_specs=(
            P(("dp", "row"), None),
            P(("dp", "row")),
            P(),
            P("row", "col"),
            P("col"),
            P("row", "col"),
            P("col"),
            P("row", "col"),
            P("col"),
            P("col", "row"),
            P(),
            P("row", "col"),
            P("row", "col"),
            P("col", "row"),
            P(("dp", "row"), None),
        ),
        out_specs=(
            P(("dp", "row"), None),
            P(("dp", "row"), None),
            P(),
            P("row", "col"),
            P("col"),
            P("row", "col"),
            P("col"),
            P("row", "col"),
            P("col"),
            P("col", "row"),
            P(),
            P("row", "col"),
            P("row", "col"),
            P("col", "row"),
        ),
        check_vma=False,
    )
```

```python
import functools

import jax
import jax.numpy as jnp
from jax import lax
from jax.experimental import pallas as pl
from jax.experimental.pallas import tpu as pltpu
from jax.sharding import PartitionSpec as P

HD = 64
HALF = HD // 2
NORM_EPS = 1e-06
ROPE_BASE = 1000000.0
NEG_BIG = -1e30
LANES = 128
EXTRA_ROWS = 16
BF16 = jnp.bfloat16
F32 = jnp.float32


def dot_rows(left, right):
    return lax.dot_general(left, right, (((0,), (0,)), ((), ())), preferred_element_type=F32)


def dot_cols(left, right):
    return lax.dot_general(left, right, (((1,), (1,)), ((), ())), preferred_element_type=F32)


def dot(left, right):
    return jnp.dot(left, right, preferred_element_type=F32)


def inverse_rms(values):
    return lax.rsqrt(jnp.mean(values * values, axis=1, keepdims=True) + NORM_EPS)


def norm_back(gradient, unit_rows, inv_rms, gain):
    scaled = gradient * gain
    inner = jnp.mean(scaled * unit_rows, axis=1, keepdims=True)
    return (inv_rms * (scaled - unit_rows * inner), jnp.sum(gradient * unit_rows, axis=0))


def after(value, *others):
    for other in others:
        first = other[(0,) * other.ndim].astype(F32)
        value = value + jnp.minimum(jnp.abs(first), 0.0).astype(value.dtype)
    return value


def swap_core(value):
    return lax.ppermute(value, "col", [(0, 1), (1, 0)])


def exchange(parts, axis):
    return lax.all_to_all(parts, axis, split_axis=0, concat_axis=0, tiled=True)


def gather(value, axis, size):
    return exchange(jnp.broadcast_to(value[None], (size,) + value.shape), axis)


def dp_send(value, step):
    pairs = []
    for group in range(4):
        for core in range(2):
            bits = 3 if step == 2 else 1 << ((step + core) % 2)
            pairs.append((group * 2 + core, (group ^ bits) * 2 + core))
    return lax.ppermute(value, ("dp", "col"), pairs)


def dp_gather(value):
    first = dp_send(value, 0)
    second = dp_send(value, 1)
    return [value, first, second, dp_send(first, 1)]


def dp_scatter_sum(parts):
    far = dp_send(parts[3].astype(BF16), 1)
    near = dp_send(after(parts[2].astype(BF16), far), 1)
    passed = (parts[1] + far.astype(F32)).astype(BF16)
    return parts[0] + near.astype(F32) + dp_send(passed, 0).astype(F32)


def pick(stacked, place):
    return lax.dynamic_index_in_dim(stacked, place, axis=0, keepdims=False)


def sum_parts(parts):
    return jnp.sum(parts.astype(F32), axis=0)


def half_turn(values):
    width = values.shape[1]
    lane = lax.broadcasted_iota(jnp.int32, values.shape, 1) % HD
    return jnp.where(
        lane < HALF, -pltpu.roll(values, width - HALF, 1), pltpu.roll(values, HALF, 1)
    )


def turned(values, cos, sin):
    copies = values.shape[1] // cos.shape[1]
    cos = jnp.concatenate([cos] * copies, axis=1)
    sin = jnp.concatenate([sin] * copies, axis=1)
    return values * cos + half_turn(values) * sin


def run(kernel, outs, *operands, scalars=(), late=(), scratch=(), flops=1, vmem=48):
    spec = pl.BlockSpec(memory_space=pltpu.VMEM)
    leads = len(scalars) + len(late)

    def body(*refs):
        kernel(*refs[: len(scalars)], *refs[leads:])

    return pl.pallas_call(
        body,
        out_shape=tuple(jax.ShapeDtypeStruct(shape, dtype) for shape, dtype in outs),
        in_specs=[pl.BlockSpec(memory_space=pltpu.SMEM)] * len(scalars)
        + [pl.BlockSpec(memory_space=pl.ANY)] * len(late)
        + [spec] * len(operands),
        out_specs=tuple([spec] * len(outs)),
        scratch_shapes=list(scratch),
        compiler_params=pltpu.CompilerParams(vmem_limit_bytes=vmem * 2**20),
        cost_estimate=pl.CostEstimate(flops=flops, bytes_accessed=2**20, transcendentals=0),
    )(*scalars, *late, *operands)


def lin_kernel(
    slot_ref, x_ref, gain_ref, bias_ref, cos_ref, sin_ref, seg_ref, *refs
):
    q_ref, kv_ref, n_ref, w_ref = refs[4:]
    count = x_ref.shape[0]
    q_width = q_ref.shape[1]
    cols = refs[0].shape[1]
    for place in range(4):
        for slot in range(4):

            @pl.when(slot_ref[place] == slot)
            def _copy(slot=slot, place=place):
                w_ref[:, place * cols : (place + 1) * cols] = refs[slot][...]

    values = x_ref[...].astype(F32)
    normed = (values * inverse_rms(values) * gain_ref[...]).astype(BF16)
    n_ref[...] = normed
    lin = dot(normed, w_ref[...])[:, q_width:] + bias_ref[...]
    rot = turned(lin[:, : q_width + HD], cos_ref[...], sin_ref[...])
    q_ref[...] = (rot[:, :q_width].astype(BF16).astype(F32) * HD ** (-0.5)).astype(BF16)
    kv = jnp.concatenate([rot[:, q_width:], lin[:, q_width + HD :]], axis=1)
    kv_ref[:count, :] = kv.astype(BF16)
    kv_ref[count:, :] = seg_ref[...]


def read_keys(kv_ref, meta_ref, bias_ref):
    rows = kv_ref.shape[0]
    count = kv_ref.shape[1] - EXTRA_ROWS
    joined_rows = jnp.concatenate([kv_ref[place, :count, :] for place in range(rows)], axis=0)
    docs = []
    for place in range(rows):
        extra = kv_ref[place, count:, :].astype(F32)
        docs += [extra[line : line + 1, :] for line in range(count // LANES)]
    key_doc = jnp.concatenate(docs, axis=1)
    key_pos = lax.broadcasted_iota(jnp.int32, (count, rows * count), 1).astype(F32)
    allowed = (key_pos <= meta_ref[:, 0:1]) & (key_doc == meta_ref[:, 1:2])
    bias_ref[...] = jnp.where(allowed, 0.0, NEG_BIG)
    return (joined_rows[:, :HD], joined_rows[:, HD:])


def attend_kernel(
    heads, q_ref, kv_ref, meta_ref, w_ref, out_ref, low_ref, lse_ref, branch_ref, bias_ref
):
    keys, values = read_keys(kv_ref, meta_ref, bias_ref)
    lane = lax.broadcasted_iota(jnp.int32, lse_ref.shape, 1)
    lse_all = jnp.zeros(lse_ref.shape, F32)
    outs = []
    for head in range(heads):
        cols = slice(head * HD, (head + 1) * HD)
        scores = dot_cols(q_ref[:, cols], keys) + bias_ref[...]
        top = jnp.max(scores, axis=1, keepdims=True)
        weights = jnp.exp(scores - top)
        total = jnp.sum(weights, axis=1, keepdims=True)
        outs.append(dot(weights.astype(BF16), values) / total)
        lse_all = jnp.where(lane == head, top + jnp.log(total), lse_all)
    heads_sum = jnp.concatenate(outs, axis=1)
    low = heads_sum.astype(BF16)
    out_ref[...] = heads_sum
    low_ref[...] = low
    lse_ref[...] = lse_all
    branch_ref[...] = dot_cols(low, w_ref[:, : heads * HD]).astype(BF16)


def norm_kernel(core_ref, x_ref, own_ref, other_ref, gain_ref, res_ref, half_ref, norm_ref):
    half = half_ref.shape[0]
    residual = x_ref[...].astype(F32) + (own_ref[...].astype(F32) + other_ref[...].astype(F32))
    res_ref[...] = residual
    norm_ref[...] = residual * inverse_rms(residual) * gain_ref[...]
    start = pl.multiple_of(core_ref[0] * half, half)
    half_ref[...] = norm_ref[pl.ds(start, half), :].astype(BF16)


def ffn_kernel(
    n_own, n_other, g_own, g_other, gate_ref, up_ref, down_ref,
    dn_own, dn_other, hidden_ref, dgate_ref, dup_ref,
):
    amount = n_own.shape[0]
    tile = min(256, amount)
    for side, n_ref, g_ref in ((1, n_other, g_other), (0, n_own, g_own)):
        for begin in range(0, amount, tile):
            part = slice(begin, begin + tile)
            normed = n_ref[part, :]
            gate = dot(normed, gate_ref[...])
            up = dot(normed, up_ref[...])
            d_hidden = dot(g_ref[part, :], down_ref[...])
            sig = 1.0 / (1.0 + jnp.exp(-gate))
            silu = gate * sig
            hidden_ref[side, part, :] = (silu * up).astype(BF16)
            d_gate = (d_hidden * up * sig * (1.0 + gate * (1.0 - sig))).astype(BF16)
            d_up = (d_hidden * silu).astype(BF16)
            dgate_ref[side, part, :] = d_gate
            dup_ref[side, part, :] = d_up
            d_normed = dot_cols(d_gate, gate_ref[...]) + dot_cols(d_up, up_ref[...])
            if side == 1:
                dn_other[part, :] = d_normed.astype(BF16)
            else:
                dn_own[part, :] = d_normed


def ffn_grad_kernel(*refs):
    out_ref = refs[-1]
    size = out_ref.shape[2]
    for item in range(out_ref.shape[1]):
        own, other, right = refs[3 * item : 3 * item + 3]
        summed = dot_rows(own[...], right[0]) + dot_rows(other[...], right[1])
        for place in range(out_ref.shape[0]):
            out_ref[place, item] = summed[place * size : (place + 1) * size].astype(BF16)


def ffn_out_kernel(hidden_ref, down_ref, own_ref, other_ref):
    other_ref[...] = dot_cols(hidden_ref[1], down_ref[...]).astype(BF16)
    own_ref[...] = dot_cols(hidden_ref[0], down_ref[...])


def back_kernel(
    heads, core_ref, dn_own, dn_other, res_ref, grad_ref, gain_ref, w_ref, cos_ref, sin_ref,
    q_ref, kv_ref, meta_ref, out_ref, lse_ref,
    dres_ref, dlow_ref, dq_ref, dkv_ref, dgain_ref, dn_ref, bias_ref,
):
    half = dn_own.shape[0]
    core = core_ref[0]
    dn_ref[pl.ds(pl.multiple_of(core * half, half), half), :] = dn_own[...].astype(F32)
    dn_ref[pl.ds(pl.multiple_of((1 - core) * half, half), half), :] = dn_other[...].astype(F32)
    d_normed = dn_ref[...]
    residual = res_ref[...]
    inv = inverse_rms(residual)
    unit = residual * inv
    d_norm, d_gain = norm_back(d_normed, unit, inv, gain_ref[...])
    dgain_ref[...] = jnp.broadcast_to(d_gain[None, :], dgain_ref.shape)
    d_res = grad_ref[...].astype(F32) + d_norm
    dres_ref[...] = d_res
    d_low = d_res.astype(BF16)
    dlow_ref[...] = d_low
    d_heads = dot(d_low, w_ref[:, : heads * HD]).astype(BF16)
    keys, values = read_keys(kv_ref, meta_ref, bias_ref)
    d_keys = jnp.zeros(keys.shape, F32)
    d_values = jnp.zeros(keys.shape, F32)
    dqs = []
    for head in range(heads):
        cols = slice(head * HD, (head + 1) * HD)
        queries = q_ref[:, cols]
        grads = d_heads[:, cols]
        delta = jnp.sum(grads.astype(F32) * out_ref[:, cols], axis=1, keepdims=True)
        scores = dot_cols(queries, keys) + bias_ref[...]
        probs = jnp.exp(scores - lse_ref[:, head : head + 1])
        d_probs = dot_cols(grads, values)
        d_scores = (probs * (d_probs - delta)).astype(BF16)
        dqs.append(dot(d_scores, keys) * HD ** (-0.5))
        d_keys = d_keys + dot_rows(d_scores, queries)
        d_values = d_values + dot_rows(probs.astype(BF16), grads)
    dqs.append(jnp.zeros_like(dqs[0]))
    dq = turned(jnp.concatenate(dqs, axis=1), cos_ref[...], -sin_ref[...])
    dq_ref[...] = dq[:, : heads * HD].astype(BF16)
    dkv = jnp.concatenate([d_keys, d_values], axis=1).astype(BF16)
    for place in range(dkv_ref.shape[0]):
        rows = dkv_ref.shape[1]
        dkv_ref[place] = dkv[place * rows : (place + 1) * rows]


def lin_back_kernel(dq_ref, dkv_ref, cos_ref, sin_ref, w_ref, parts_ref, dn_ref):
    dkv = dkv_ref[0].astype(F32)
    for place in range(1, dkv_ref.shape[0]):
        dkv = dkv + dkv_ref[place].astype(F32)
    d_key = turned(dkv, cos_ref[...], -sin_ref[...])
    d_lin = jnp.concatenate(
        [dq_ref[...], d_key[:, :HD].astype(BF16), dkv[:, HD:].astype(BF16)], axis=1
    )
    cols = parts_ref.shape[2]
    for place in range(4):
        parts_ref[place] = d_lin[:, place * cols : (place + 1) * cols]
    nothing = jnp.zeros(dq_ref.shape, BF16)
    dn_ref[...] = dot_cols(jnp.concatenate([nothing, d_lin], axis=1), w_ref[...]).astype(BF16)


def final_kernel(x_ref, own_ref, other_ref, gain_ref, dres_ref, grad_ref, dgain_ref):
    d_normed = own_ref[...].astype(F32) + other_ref[...].astype(F32)
    values = x_ref[...].astype(F32)
    inv = inverse_rms(values)
    d_norm, d_gain = norm_back(d_normed, values * inv, inv, gain_ref[...])
    grad_ref[...] = (dres_ref[...] + d_norm).astype(BF16)
    dgain_ref[...] = jnp.broadcast_to(d_gain[None, :], dgain_ref.shape)


def lin_grad_kernel(target_ref, *refs):
    d_lin_ref, out_ref, pack_ref, bias_ref = refs[4:]
    summed = bias = None
    for place in range(4):
        block = d_lin_ref[target_ref[place]]
        part = dot_rows(refs[place][...], block)
        part_bias = jnp.sum(block.astype(F32), axis=0, keepdims=True)
        summed = part if summed is None else summed + part
        bias = part_bias if bias is None else bias + part_bias
    pack_ref[...] = jnp.concatenate([out_ref[...].T, summed], axis=1).astype(BF16)
    bias_ref[...] = jnp.broadcast_to(bias, bias_ref.shape)


def place_kernel(parts, row_ref, *refs):
    rows = len(refs) - parts
    for step in range(rows):
        size = refs[step].shape[0] // parts
        place = (row_ref[0] + rows - step) % rows
        for part in range(parts):
            refs[rows + part][place] = refs[step][part * size : (part + 1) * size, :]


def place_rows(row, late, pieces, parts=1):
    size = pieces[0].shape[0] // parts
    shape = (len(pieces), size, pieces[0].shape[1])
    placed = run(
        functools.partial(place_kernel, parts),
        [(shape, BF16)] * parts,
        *pieces,
        scalars=(row[None].astype(jnp.int32),),
        late=(late,),
        vmem=32,
    )
    return [out.reshape(-1, out.shape[2]) for out in placed]


def join_kernel(slot_ref, *refs):
    amount = len(refs)
    groups = 0
    while 4 * groups + sum(refs[4 * i].shape[0] for i in range(groups)) < amount:
        groups += 1
    outs = refs[4 * groups :]
    index = 0
    for number in range(groups):
        blocks = refs[4 * number : 4 * number + 4]
        cols = blocks[0].shape[2]
        for item in range(blocks[0].shape[0]):
            for place in range(4):
                for slot in range(4):

                    @pl.when(slot_ref[place] == slot)
                    def _copy(index=index, item=item, slot=slot, place=place, blocks=blocks):
                        value = blocks[slot][item].astype(F32)
                        outs[index][:, place * cols : (place + 1) * cols] = value

            index += 1


def join(slots, *groups):
    return run(
        join_kernel,
        [
            ((group[0].shape[1], 4 * group[0].shape[2]), F32)
            for group in groups
            for _ in range(group[0].shape[0])
        ],
        *[block for group in groups for block in group],
        scalars=(slots,),
        vmem=32,
    )


def attn_join_kernel(out_cols, part_ref, out_ref, query_ref, key_ref, value_ref):
    d_rows = query_ref.shape[0]
    parts = [part_ref[place, :d_rows, :].astype(F32) for place in range(4)]
    out_ref[...] = jnp.concatenate([part[:, :out_cols] for part in parts], axis=1).T
    lin = jnp.concatenate([part[:, out_cols:] for part in parts], axis=1)
    q_width = query_ref.shape[1]
    query_ref[...] = lin[:, :q_width]
    key_ref[...] = lin[:, q_width : q_width + HD].T
    value_ref[...] = lin[:, q_width + HD :].T


def per_device(
    rows,
    tokens,
    segment_ids,
    attn_gain,
    w_query,
    b_query,
    w_key,
    b_key,
    w_value,
    b_value,
    w_out,
    ffn_gain,
    w_gate,
    w_up,
    w_down,
    out_grad,
):
    count, width = tokens.shape
    half = count // 2
    d_rows = w_query.shape[0]
    q_width = w_query.shape[1]
    qk_width = q_width + HD
    lin_width = qk_width + HD
    heads = q_width // HD
    units = w_gate.shape[1] // 4
    row = lax.axis_index("row")
    group = lax.axis_index("dp")
    core = lax.axis_index("col")

    targets = [group, group ^ (1 + core), group ^ (2 - core), group ^ 3]
    slots = []
    for place in range(4):
        relative = group ^ place
        flipped = (relative & 1) * 2 + (relative >> 1)
        slots.append(jnp.where(core == 0, relative, flipped))
    slots = jnp.stack(slots).astype(jnp.int32)
    target_numbers = jnp.stack(targets).astype(jnp.int32)
    core_number = core[None].astype(jnp.int32)

    around = [(i, (i + 1) % rows) for i in range(rows)]

    def ring_spread(own):
        pieces = [own]
        for _ in range(1, rows):
            pieces.append(lax.ppermute(pieces[-1], "row", around))
        return pieces

    def ring_sum(parts, *lates):
        moving = pick(parts, (row + rows - 1) % rows)
        for step in range(2, rows + 1):
            arrived = lax.ppermute(moving, "row", around).astype(F32)
            summed = arrived + pick(parts, (row + rows - step) % rows).astype(F32)
            moving = after(summed, *lates[step - 2 : step - 1]).astype(BF16)
        return moving

    with jax.named_scope("attn_weights"):
        block = jnp.concatenate([w_out.T, w_query, w_key, w_value], axis=1)
        block_cols = block.shape[1] // 4
        own_quarter = lax.dynamic_slice_in_dim(block, group * block_cols, block_cols, axis=1)
        quarters = gather(own_quarter, "row", rows).reshape(width, block_cols)
        w_blocks = dp_gather(quarters)

    def split_gather(own, *late):
        own = after(jnp.concatenate(dp_gather(own), axis=0), *late)
        return (own, swap_core(own))

    def split_scatter_sum(own, other):
        moved = swap_core(other)
        blocks = moved.reshape(4, half, width)
        own = own.reshape(4, half, width)
        parts = [own[place] + blocks[place].astype(F32) for place in range(4)]
        far = dp_send(parts[3].astype(BF16), 1)
        near = dp_send(after(parts[2].astype(BF16), far), 1)
        passed = dp_send((parts[1] + far.astype(F32)).astype(BF16), 0)
        done = (parts[0] + near.astype(F32) + passed.astype(F32)).astype(BF16)
        return (done, swap_core(done), moved, far)

    gain_one = attn_gain.astype(F32)[None, :]
    gain_two = ffn_gain.astype(F32)[None, :]
    bias = jnp.concatenate([b_query, b_key, b_value]).astype(F32)[None, :]
    positions = (row * count + jnp.arange(count, dtype=jnp.int32)).astype(F32)
    ladder = (jnp.arange(2 * HD, dtype=jnp.int32) % HALF).astype(F32) * (2.0 / HD)
    angles = positions[:, None] * jnp.exp(-ladder * jnp.log(ROPE_BASE))[None, :]
    cos_table, sin_table = jnp.cos(angles), jnp.sin(angles)
    seg_rows = count // LANES
    seg_own = segment_ids.astype(BF16).reshape(seg_rows, LANES)
    seg_own = jnp.pad(seg_own, ((0, EXTRA_ROWS - seg_rows), (0, 0)))
    query_meta = jnp.stack([positions, segment_ids.astype(F32)], axis=1)
    with jax.named_scope("lin"):
        queries, kv_own, normed1, w_attn = run(
            lin_kernel,
            [
                ((count, q_width), BF16),
                ((count + EXTRA_ROWS, 2 * HD), BF16),
                ((count, width), BF16),
                ((width, 4 * block_cols), BF16),
            ],
            tokens, gain_one, bias, cos_table, sin_table, seg_own, *w_blocks,
            scalars=(slots,),
        )
    with jax.named_scope("kv_move"):
        kv_all = gather(kv_own, "row", rows)
    with jax.named_scope("out_grad_gather"):
        own_grad = lax.dynamic_slice_in_dim(out_grad, core * half, half, axis=0)
        grad_own, grad_other = split_gather(after(own_grad, w_blocks[3]))
    with jax.named_scope("normed1_gather"):
        normed1_all = dp_gather(after(normed1, grad_other))
    with jax.named_scope("ffn_weights"):
        own_ffn = jnp.concatenate(
            [
                lax.dynamic_slice_in_dim(w_gate, group * units, units, axis=1),
                lax.dynamic_slice_in_dim(w_up, group * units, units, axis=1),
                lax.dynamic_slice_in_dim(w_down, group * units, units, axis=0).T,
            ],
            axis=0,
        )
        ffn_pieces = ring_spread(after(own_ffn, quarters))

    key_count = rows * count
    with jax.named_scope("attention"):
        attn_out, attn_heads, log_sum, branch = run(
            functools.partial(attend_kernel, heads),
            [
                ((count, q_width), F32),
                ((count, q_width), BF16),
                ((count, LANES), F32),
                ((count, width), BF16),
            ],
            queries, kv_all, query_meta, w_attn,
            late=(ffn_pieces[1],),
            scratch=[pltpu.VMEM((count, key_count), F32)],
        )
        residual, normed2 = run(
            norm_kernel,
            [((count, width), F32), ((half, width), BF16)],
            tokens, branch, swap_core(branch), gain_two,
            scalars=(core_number,),
            late=(grad_other, normed1_all[3], ffn_pieces[2]),
            scratch=[pltpu.VMEM((count, width), F32)],
        )

    with jax.named_scope("normed2_gather"):
        normed_own, normed_other = split_gather(normed2, ffn_pieces[-1])
    with jax.named_scope("ffn_weights"):
        ffn_w = place_rows(row, normed2, ffn_pieces, parts=3)
    amount = 4 * half
    wide = ((2, amount, units), BF16)
    with jax.named_scope("ffn"):
        dn_own, dn_other, hidden, d_gate, d_up = run(
            ffn_kernel,
            [((amount, width), F32), ((amount, width), BF16), wide, wide, wide],
            normed_own, normed_other, grad_own, grad_other, *ffn_w,
            flops=10**9,
        )
    with jax.named_scope("d_normed2_sum"):
        d_normed_own, d_normed_other, moved, far = split_scatter_sum(dn_own, dn_other)
    with jax.named_scope("ffn_grads"):
        (pair_grads,) = run(
            ffn_grad_kernel,
            [((rows, 2, d_rows, units), BF16)],
            normed_own, normed_other, d_up, grad_own, grad_other, hidden,
            late=(moved,),
            flops=10**9,
        )
        (gate_grads,) = run(
            ffn_grad_kernel,
            [((rows, 1, d_rows, units), BF16)],
            normed_own, normed_other, d_gate,
            late=(far,),
            flops=10**9,
        )

    with jax.named_scope("attention_back"):
        d_residual, d_low, dq, dkv_parts, d_gain_two = run(
            functools.partial(back_kernel, heads),
            [
                ((count, width), F32),
                ((count, width), BF16),
                ((count, q_width), BF16),
                ((rows, count, 2 * HD), BF16),
                ((8, width), F32),
            ],
            d_normed_own, d_normed_other, residual, out_grad, gain_two, w_attn, cos_table,
            sin_table, queries, kv_all, query_meta, attn_out, log_sum,
            scalars=(core_number,),
            late=(gate_grads, pair_grads),
            scratch=[pltpu.VMEM((count, width), F32), pltpu.VMEM((count, key_count), F32)],
        )
    with jax.named_scope("dkv_move"):
        dkv = exchange(dkv_parts, "row")
    with jax.named_scope("out_grads"):
        out_cols = q_width // 4
        out_part = dot_rows(attn_heads, d_low).reshape(4, out_cols, width)
        out_sum = dp_scatter_sum([pick(out_part, target) for target in targets])
    with jax.named_scope("d_lin"):
        lin_cols = lin_width // 4
        d_lin_parts, d_normed1 = run(
            lin_back_kernel,
            [((4, count, lin_cols), BF16), ((count, width), BF16)],
            dq, dkv, cos_table, sin_table, w_attn,
            late=(out_sum,),
        )
        d_lin_all = exchange(d_lin_parts, "dp")
    with jax.named_scope("ffn_grad_rows"):
        gate_sum = ring_sum(gate_grads, d_normed_other, dq, dkv)
        pair_sum = ring_sum(pair_grads, dq, dkv, d_lin_parts)
    with jax.named_scope("d_normed1"):
        grad_tokens, d_gain_one = run(
            final_kernel,
            [((count, width), BF16), ((8, width), F32)],
            tokens, d_normed1, swap_core(d_normed1), gain_one, d_residual,
        )
    with jax.named_scope("ffn_branch_sum"):
        branch_own, branch_other = run(
            ffn_out_kernel,
            [((amount, width), F32), ((amount, width), BF16)],
            hidden, ffn_w[2],
            late=(out_sum,),
        )
        own, other = split_scatter_sum(branch_own, branch_other)[:2]
        low = jnp.where(core == 0, own, other).astype(F32)
        high = jnp.where(core == 0, other, own).astype(F32)
        output = (residual + jnp.concatenate([low, high], axis=0)).astype(BF16)
    with jax.named_scope("ffn_grad_groups"):
        gate_done = dp_gather(gate_sum)

    pack_width = out_cols + lin_cols
    with jax.named_scope("lin_grads"):
        attn_grads, bias_sum = run(
            lin_grad_kernel,
            [((width, pack_width), BF16), ((8, lin_cols), F32)],
            *normed1_all, d_lin_all, out_sum,
            scalars=(target_numbers,),
        )
    small = jnp.concatenate([d_gain_one[0], d_gain_two[0], bias_sum[0]])
    small = jnp.pad(small, (0, EXTRA_ROWS // 2 * pack_width - small.shape[0]))

    def two_halves(values):
        high = values.astype(BF16)
        low = (values - high.astype(F32)).astype(BF16)
        return jnp.concatenate([high, low]).reshape(EXTRA_ROWS, pack_width)

    def whole(pair):
        return pair[: EXTRA_ROWS // 2].astype(F32) + pair[EXTRA_ROWS // 2 :].astype(F32)

    attn_grads = jnp.concatenate(
        [
            attn_grads.reshape(rows, d_rows, pack_width),
            jnp.broadcast_to(two_halves(small), (rows, EXTRA_ROWS, pack_width)),
        ],
        axis=1,
    )
    with jax.named_scope("attn_grad_rows"):
        received = exchange(attn_grads, "row")
        attn_sum = sum_parts(received[:, :d_rows]).astype(BF16)
        small_sum = whole(received[0, d_rows:])
        for place in range(1, rows):
            small_sum = small_sum + whole(received[place, d_rows:])
    with jax.named_scope("ffn_grad_groups"):
        pair_done = dp_gather(pair_sum)
    with jax.named_scope("attn_grad_groups"):
        attn_done = gather(
            jnp.concatenate([attn_sum, two_halves(small_sum.reshape(-1))], axis=0), "dp", 4
        )
    with jax.named_scope("joins"):
        grad_w_gate, grad_w_up, grad_w_down_t = join(slots, gate_done, pair_done)
        grad_w_out, grad_w_query, grad_w_key, grad_w_value = run(
            functools.partial(attn_join_kernel, out_cols),
            [
                ((q_width, d_rows), F32),
                ((d_rows, q_width), F32),
                ((HD, d_rows), F32),
                ((HD, d_rows), F32),
            ],
            attn_done,
        )
    smalls = [whole(attn_done[place, d_rows:]).reshape(-1) for place in range(4)]
    gains = smalls[0][: 2 * width]
    for small_piece in smalls[1:]:
        gains = gains + small_piece[: 2 * width]
    biases = jnp.concatenate(
        [small_piece[2 * width : 2 * width + lin_cols] for small_piece in smalls]
    )
    return (
        output,
        grad_tokens,
        gains[:width],
        grad_w_query,
        biases[:q_width],
        grad_w_key.T,
        biases[q_width:qk_width],
        grad_w_value.T,
        biases[qk_width:],
        grad_w_out,
        gains[width:],
        grad_w_gate,
        grad_w_up,
        grad_w_down_t.T,
    )


def solution(mesh):
    return jax.shard_map(
        functools.partial(per_device, mesh.shape["row"]),
        mesh=mesh,
        in_specs=(
            P(("dp", "row"), None),
            P(("dp", "row")),
            P(),
            P("row", "col"),
            P("col"),
            P("row", "col"),
            P("col"),
            P("row", "col"),
            P("col"),
            P("col", "row"),
            P(),
            P("row", "col"),
            P("row", "col"),
            P("col", "row"),
            P(("dp", "row"), None),
        ),
        out_specs=(
            P(("dp", "row"), None),
            P(("dp", "row"), None),
            P(),
            P("row", "col"),
            P("col"),
            P("row", "col"),
            P("col"),
            P("row", "col"),
            P("col"),
            P("col", "row"),
            P(),
            P("row", "col"),
            P("row", "col"),
            P("col", "row"),
        ),
        check_vma=False,
    )
```

```python
import functools

import jax
import jax.numpy as jnp
from jax import lax
from jax.experimental import pallas as pl
from jax.experimental.pallas import tpu as pltpu
from jax.sharding import PartitionSpec as P

HD = 64
HALF = HD // 2
NORM_EPS = 1e-06
ROPE_BASE = 1000000.0
NEG_BIG = -1e30
LANES = 128
EXTRA_ROWS = 16
BF16 = jnp.bfloat16
F32 = jnp.float32


def dot_rows(left, right):
    return lax.dot_general(left, right, (((0,), (0,)), ((), ())), preferred_element_type=F32)


def dot_cols(left, right):
    return lax.dot_general(left, right, (((1,), (1,)), ((), ())), preferred_element_type=F32)


def dot(left, right):
    return jnp.dot(left, right, preferred_element_type=F32)


def inverse_rms(values):
    return lax.rsqrt(jnp.mean(values * values, axis=1, keepdims=True) + NORM_EPS)


def norm_back(gradient, unit_rows, inv_rms, gain):
    scaled = gradient * gain
    inner = jnp.mean(scaled * unit_rows, axis=1, keepdims=True)
    return (inv_rms * (scaled - unit_rows * inner), jnp.sum(gradient * unit_rows, axis=0))


def after(value, *others):
    for other in others:
        first = other[(0,) * other.ndim].astype(F32)
        value = value + jnp.minimum(jnp.abs(first), 0.0).astype(value.dtype)
    return value


def swap_core(value):
    return lax.ppermute(value, "col", [(0, 1), (1, 0)])


def exchange(parts, axis):
    return lax.all_to_all(parts, axis, split_axis=0, concat_axis=0, tiled=True)


def gather(value, axis, size):
    return exchange(jnp.broadcast_to(value[None], (size,) + value.shape), axis)


def dp_send(value, step):
    pairs = []
    for group in range(4):
        for core in range(2):
            bits = 3 if step == 2 else 1 << ((step + core) % 2)
            pairs.append((group * 2 + core, (group ^ bits) * 2 + core))
    return lax.ppermute(value, ("dp", "col"), pairs)


def dp_gather(value):
    return [value] + [dp_send(value, step) for step in range(3)]


def dp_gather_wide(value):
    first, second = dp_send(value, 0), dp_send(value, 1)
    half = value.shape[0] // 2
    passed = (first[:half], second[half:])
    far = jnp.concatenate([dp_send(passed[0], 1), dp_send(passed[1], 0)], axis=0)
    return ([value, first, second, far], passed)


def dp_scatter_sum(parts):
    moved = [dp_send(part.astype(BF16), step) for step, part in enumerate(parts[1:])]
    return parts[0] + moved[0].astype(F32) + moved[1].astype(F32) + moved[2].astype(F32)


def pick(stacked, place):
    return lax.dynamic_index_in_dim(stacked, place, axis=0, keepdims=False)


def sum_parts(parts):
    return jnp.sum(parts.astype(F32), axis=0)


def half_turn(values):
    width = values.shape[1]
    lane = lax.broadcasted_iota(jnp.int32, values.shape, 1) % HD
    return jnp.where(
        lane < HALF, -pltpu.roll(values, width - HALF, 1), pltpu.roll(values, HALF, 1)
    )


def turned(values, cos, sin):
    copies = values.shape[1] // cos.shape[1]
    cos = jnp.concatenate([cos] * copies, axis=1)
    sin = jnp.concatenate([sin] * copies, axis=1)
    return values * cos + half_turn(values) * sin


def run(
    kernel, outs, *operands, scalars=(), late=(), far=(), scratch=(), flops=1, load=False, vmem=48
):
    leads = len(scalars) + len(late)
    first = leads + len(far)
    amount = len(operands)
    spec = pl.BlockSpec(memory_space=pltpu.VMEM)
    anywhere = pl.BlockSpec(memory_space=pl.ANY)

    def body(*refs):
        held, rest = refs[first : first + amount], refs[first + amount :]
        if load:
            sources, held, sems = held, rest[len(rest) - amount - 1 : -1], rest[-1]
            rest = rest[: len(rest) - amount - 1]
            copies = [
                pltpu.make_async_copy(source, place, sems.at[number])
                for number, (source, place) in enumerate(zip(sources, held))
            ]
            for copy in copies:
                copy.start()
            for copy in copies:
                copy.wait()
        kernel(*refs[: len(scalars)], *refs[leads:first], *held, *rest)

    places = [pltpu.VMEM(operand.shape, operand.dtype) for operand in operands] if load else []
    return pl.pallas_call(
        body,
        out_shape=tuple(jax.ShapeDtypeStruct(shape, dtype) for shape, dtype in outs),
        in_specs=[pl.BlockSpec(memory_space=pltpu.SMEM)] * len(scalars)
        + [anywhere] * (len(late) + len(far))
        + [anywhere if load else spec] * amount,
        out_specs=tuple([spec] * len(outs)),
        scratch_shapes=list(scratch)
        + places
        + ([pltpu.SemaphoreType.DMA((amount,))] if load else []),
        compiler_params=pltpu.CompilerParams(vmem_limit_bytes=vmem * 2**20),
        cost_estimate=pl.CostEstimate(flops=flops, bytes_accessed=2**20, transcendentals=0),
    )(*scalars, *late, *far, *operands)


def copy_kernel(*refs):
    out_ref = refs[-1]
    begin = 0
    for ref in refs[:-1]:
        out_ref[begin : begin + ref.shape[0], :] = ref[...]
        begin += ref.shape[0]


def stacked(blocks, *late):
    amount = sum(block.shape[0] for block in blocks)
    return run(
        copy_kernel, [((amount, blocks[0].shape[1]), blocks[0].dtype)], *blocks, late=late, vmem=32
    )[0]


def parts_kernel(*refs):
    out_ref = refs[-1]
    if len(refs) == 2:
        out_ref[...] = refs[0][...]
    else:
        for part, ref in enumerate(refs[:-1]):
            out_ref[part] = ref[...]


def place_kernel(row_ref, *refs):
    out_ref = refs[-1]
    rows = len(refs) - 1
    for step in range(rows):
        out_ref[(row_ref[0] + rows - step) % rows] = refs[step][...]


def sum_kernel(own_ref, first_ref, second_ref, both_ref, out_ref):
    summed = own_ref[...] + first_ref[...].astype(F32) + second_ref[...].astype(F32)
    out_ref[...] = (summed + both_ref[...].astype(F32)).astype(BF16)


def core_sum_kernel(target_ref, own_ref, moved_ref, out_ref):
    half = out_ref.shape[1]
    for place in range(4):
        part = slice(place * half, (place + 1) * half)
        summed = own_ref[part, :] + moved_ref[part, :].astype(F32)
        out_ref[target_ref[place]] = summed.astype(BF16)


def sum_four_kernel(parts_ref, out_ref):
    summed = parts_ref[0].astype(F32)
    for place in range(1, 4):
        summed = summed + parts_ref[place].astype(F32)
    out_ref[...] = summed.astype(BF16)


def ring_add_kernel(place_ref, parts_ref, moved_ref, out_ref, block_ref, sem):
    copy = pltpu.make_async_copy(parts_ref.at[place_ref[0]], block_ref, sem)
    copy.start()
    copy.wait()
    out_ref[...] = (moved_ref[...].astype(F32) + block_ref[...].astype(F32)).astype(BF16)


def lin_kernel(
    slot_ref, n_ref, bias_ref, cos_ref, sin_ref, seg_ref, *refs
):
    q_ref, kv_ref, w_ref = refs[4:]
    count = n_ref.shape[0]
    q_width = q_ref.shape[1]
    cols = refs[0].shape[1]
    for place in range(4):
        for slot in range(4):

            @pl.when(slot_ref[place] == slot)
            def _copy(slot=slot, place=place):
                w_ref[:, place * cols : (place + 1) * cols] = refs[slot][...]

    lin = dot(n_ref[...], w_ref[...])[:, q_width:] + bias_ref[...]
    rot = turned(lin[:, : q_width + HD], cos_ref[...], sin_ref[...])
    q_ref[...] = (rot[:, :q_width].astype(BF16).astype(F32) * HD ** (-0.5)).astype(BF16)
    kv = jnp.concatenate([rot[:, q_width:], lin[:, q_width + HD :]], axis=1)
    kv_ref[:count, :] = kv.astype(BF16)
    kv_ref[count:, :] = seg_ref[...]


def read_keys(kv_refs, meta_ref, pos_ref, bias_ref):
    count = kv_refs[0].shape[0] - EXTRA_ROWS
    joined_rows = jnp.concatenate([ref[:count, :] for ref in kv_refs], axis=0)
    docs = []
    for ref in kv_refs:
        extra = ref[count:, :].astype(F32)
        docs += [extra[line : line + 1, :] for line in range(count // LANES)]
    key_doc = jnp.concatenate(docs, axis=1)
    allowed = (pos_ref[0:1, :] <= meta_ref[:, 0:1]) & (key_doc == meta_ref[:, 1:2])
    bias_ref[...] = jnp.where(allowed, 0.0, NEG_BIG)
    return (joined_rows[:, :HD], joined_rows[:, HD:])


def attend_kernel(heads, q_ref, meta_ref, pos_ref, w_ref, *refs):
    out_ref, low_ref, lse_ref, branch_ref, bias_ref = refs[-5:]
    keys, values = read_keys(refs[:-5], meta_ref, pos_ref, bias_ref)
    lane = lax.broadcasted_iota(jnp.int32, lse_ref.shape, 1)
    lse_all = jnp.zeros(lse_ref.shape, F32)
    outs = []
    for head in range(heads):
        cols = slice(head * HD, (head + 1) * HD)
        scores = dot_cols(q_ref[:, cols], keys) + bias_ref[...]
        top = jnp.max(scores, axis=1, keepdims=True)
        weights = jnp.exp(scores - top)
        total = jnp.sum(weights, axis=1, keepdims=True)
        outs.append(dot(weights.astype(BF16), values) / total)
        lse_all = jnp.where(lane == head, top + jnp.log(total), lse_all)
    heads_sum = jnp.concatenate(outs, axis=1)
    low = heads_sum.astype(BF16)
    out_ref[...] = heads_sum
    low_ref[...] = low
    lse_ref[...] = lse_all
    branch_ref[...] = dot_cols(low, w_ref[:, : heads * HD]).astype(BF16)


def norm_kernel(core_ref, x_ref, own_ref, other_ref, gain_ref, res_ref, half_ref, norm_ref):
    half = half_ref.shape[0]
    residual = x_ref[...].astype(F32) + (own_ref[...].astype(F32) + other_ref[...].astype(F32))
    res_ref[...] = residual
    norm_ref[...] = residual * inverse_rms(residual) * gain_ref[...]
    start = pl.multiple_of(core_ref[0] * half, half)
    half_ref[...] = norm_ref[pl.ds(start, half), :].astype(BF16)


def ffn_kernel(
    n_own, n_other, g_own, g_other, w_ref,
    dn_own, dn_other, hidden_ref, dgate_ref, dup_ref, gate_ref, up_ref, down_ref,
):
    size = w_ref.shape[2]
    for place in range(w_ref.shape[0]):
        for part, ref in enumerate((gate_ref, up_ref, down_ref)):
            ref[place * size : (place + 1) * size, :] = w_ref[place, part]
    ffn_math(
        n_own, n_other, g_own, g_other, gate_ref, up_ref, down_ref,
        dn_own, dn_other, hidden_ref, dgate_ref, dup_ref,
    )


def ffn_math(
    n_own, n_other, g_own, g_other, gate_ref, up_ref, down_ref,
    dn_own, dn_other, hidden_ref, dgate_ref, dup_ref,
):
    amount = n_own.shape[0]
    tile = min(256, amount)
    for side, n_ref, g_ref in ((1, n_other, g_other), (0, n_own, g_own)):
        for begin in range(0, amount, tile):
            part = slice(begin, begin + tile)
            normed = n_ref[part, :]
            gate = dot(normed, gate_ref[...])
            up = dot(normed, up_ref[...])
            d_hidden = dot(g_ref[part, :], down_ref[...])
            sig = 1.0 / (1.0 + jnp.exp(-gate))
            silu = gate * sig
            hidden_ref[side, part, :] = (silu * up).astype(BF16)
            d_gate = (d_hidden * up * sig * (1.0 + gate * (1.0 - sig))).astype(BF16)
            d_up = (d_hidden * silu).astype(BF16)
            dgate_ref[side, part, :] = d_gate
            dup_ref[side, part, :] = d_up
            d_normed = dot_cols(d_gate, gate_ref[...]) + dot_cols(d_up, up_ref[...])
            if side == 1:
                dn_other[part, :] = d_normed.astype(BF16)
            else:
                dn_own[part, :] = d_normed


def ffn_grad_kernel(first_ref, *refs):
    out_ref, begin_ref = refs[-2:]
    size = out_ref.shape[2]
    for item in range(out_ref.shape[1]):
        own, other, right = refs[3 * item : 3 * item + 3]
        summed = dot_rows(own[...], right[0]) + dot_rows(other[...], right[1])
        for place in range(out_ref.shape[0]):
            out_ref[place, item] = summed[place * size : (place + 1) * size].astype(BF16)
    begin_ref[...] = out_ref[first_ref[0]]


def out_grad_kernel(heads_ref, low_ref, out_ref):
    cols = out_ref.shape[1]
    product = dot_rows(heads_ref[...], low_ref[...])
    for place in range(4):
        out_ref[place] = product[place * cols : (place + 1) * cols].astype(BF16)


def ffn_out_kernel(hidden_ref, w_ref, own_ref, other_ref, down_ref):
    size = w_ref.shape[2]
    for place in range(w_ref.shape[0]):
        down_ref[place * size : (place + 1) * size, :] = w_ref[place, 2]
    other_ref[...] = dot_cols(hidden_ref[1], down_ref[...]).astype(BF16)
    own_ref[...] = dot_cols(hidden_ref[0], down_ref[...])


def back_kernel(
    heads, core_ref, dn_own, dn_other, res_ref, grad_ref, gain_ref, w_ref, cos_ref, sin_ref,
    q_ref, meta_ref, pos_ref, out_ref, lse_ref, *refs,
):
    rows = (len(refs) - 6) // 2
    dres_ref, dlow_ref, dq_ref, dgain_ref = refs[rows : rows + 4]
    dkv_refs = refs[rows + 4 : 2 * rows + 4]
    dn_ref, bias_ref = refs[-2:]
    half = dn_own.shape[0]
    core = core_ref[0]
    dn_ref[pl.ds(pl.multiple_of(core * half, half), half), :] = dn_own[...].astype(F32)
    dn_ref[pl.ds(pl.multiple_of((1 - core) * half, half), half), :] = dn_other[...].astype(F32)
    d_normed = dn_ref[...]
    residual = res_ref[...]
    inv = inverse_rms(residual)
    unit = residual * inv
    d_norm, d_gain = norm_back(d_normed, unit, inv, gain_ref[...])
    dgain_ref[...] = jnp.broadcast_to(d_gain[None, :], dgain_ref.shape)
    d_res = grad_ref[...].astype(F32) + d_norm
    dres_ref[...] = d_res
    d_low = d_res.astype(BF16)
    dlow_ref[...] = d_low
    d_heads = dot(d_low, w_ref[:, : heads * HD]).astype(BF16)
    keys, values = read_keys(refs[:rows], meta_ref, pos_ref, bias_ref)
    d_keys = jnp.zeros(keys.shape, F32)
    d_values = jnp.zeros(keys.shape, F32)
    dqs = []
    for head in range(heads):
        cols = slice(head * HD, (head + 1) * HD)
        queries = q_ref[:, cols]
        grads = d_heads[:, cols]
        delta = jnp.sum(grads.astype(F32) * out_ref[:, cols], axis=1, keepdims=True)
        scores = dot_cols(queries, keys) + bias_ref[...]
        probs = jnp.exp(scores - lse_ref[:, head : head + 1])
        d_probs = dot_cols(grads, values)
        d_scores = (probs * (d_probs - delta)).astype(BF16)
        dqs.append(dot(d_scores, keys) * HD ** (-0.5))
        d_keys = d_keys + dot_rows(d_scores, queries)
        d_values = d_values + dot_rows(probs.astype(BF16), grads)
    dqs.append(jnp.zeros_like(dqs[0]))
    dq = turned(jnp.concatenate(dqs, axis=1), cos_ref[...], -sin_ref[...])
    dq_ref[...] = dq[:, : heads * HD].astype(BF16)
    dkv = jnp.concatenate([d_keys, d_values], axis=1).astype(BF16)
    count = dkv_refs[0].shape[0]
    for place, ref in enumerate(dkv_refs):
        ref[...] = dkv[place * count : (place + 1) * count]


def lin_back_kernel(target_ref, dq_ref, cos_ref, sin_ref, w_ref, n_ref, *refs):
    dn_ref, bias_ref = refs[-7:-5]
    blocks, product_ref = refs[-5:-1], refs[-1]
    dkv = refs[0][...].astype(F32)
    for ref in refs[1:-7]:
        dkv = dkv + ref[...].astype(F32)
    d_key = turned(dkv, cos_ref[...], -sin_ref[...])
    d_lin = jnp.concatenate(
        [dq_ref[...], d_key[:, :HD].astype(BF16), dkv[:, HD:].astype(BF16)], axis=1
    )
    product_ref[...] = dot_rows(d_lin, n_ref[...])
    cols = blocks[0].shape[0]
    for place, ref in enumerate(blocks):
        begin = pl.multiple_of(target_ref[place] * cols, cols)
        ref[...] = product_ref[pl.ds(begin, cols), :].astype(ref.dtype)
    nothing = jnp.zeros(dq_ref.shape, BF16)
    dn_ref[...] = dot_cols(jnp.concatenate([nothing, d_lin], axis=1), w_ref[...]).astype(BF16)
    bias = jnp.sum(d_lin.astype(F32), axis=0, keepdims=True)
    bias_ref[...] = jnp.broadcast_to(bias, bias_ref.shape)


def final_kernel(x_ref, own_ref, other_ref, gain_ref, dres_ref, grad_ref, dgain_ref):
    d_normed = own_ref[...].astype(F32) + other_ref[...].astype(F32)
    values = x_ref[...].astype(F32)
    inv = inverse_rms(values)
    d_norm, d_gain = norm_back(d_normed, values * inv, inv, gain_ref[...])
    grad_ref[...] = (dres_ref[...] + d_norm).astype(BF16)
    dgain_ref[...] = jnp.broadcast_to(d_gain[None, :], dgain_ref.shape)


def packet_kernel(row_ref, gain_one, gain_two, bias_ref, *refs):
    pack_ref = refs[-1]
    packets = refs[5:-1]
    out_ref = refs[0]
    out_sum = out_ref[0].astype(F32)
    for place in range(1, 4):
        out_sum = out_sum + out_ref[place].astype(F32)
    lin_sum = refs[1][...]
    for ref in refs[2:5]:
        lin_sum = lin_sum + ref[...].astype(F32)
    pack_ref[...] = jnp.concatenate([out_sum, lin_sum], axis=0).T
    cols = pack_ref.shape[1]
    lines = []
    for ref in (gain_one, gain_two, bias_ref):
        values = ref[0:1, :]
        spare = -values.shape[1] % cols
        values = jnp.concatenate([values, jnp.zeros((1, spare), F32)], axis=1)
        lines += [values[:, at : at + cols] for at in range(0, values.shape[1], cols)]
    lines.append(jnp.zeros((EXTRA_ROWS - len(lines), cols), F32))
    small = jnp.concatenate(lines, axis=0).astype(BF16)
    rows = len(packets)
    size = pack_ref.shape[0] // rows
    for step, packet in enumerate(packets):
        begin = pl.multiple_of(((row_ref[0] + step) % rows) * size, size)
        packet[:EXTRA_ROWS, :] = small
        packet[EXTRA_ROWS:, :] = pack_ref[pl.ds(begin, size), :].astype(BF16)


def packet_sum_kernel(row_ref, *refs):
    rows = len(refs) - 2
    out_ref, small_ref = refs[-2:]
    summed = refs[0][EXTRA_ROWS:, :].astype(F32)
    for ref in refs[1:rows]:
        summed = summed + ref[EXTRA_ROWS:, :].astype(F32)
    for step in range(rows):
        small_ref[(row_ref[0] + rows - step) % rows] = refs[step][:EXTRA_ROWS, :].astype(F32)
    small = small_ref[0]
    for place in range(1, rows):
        small = small + small_ref[place]
    out_ref[:EXTRA_ROWS, :] = small.astype(BF16)
    out_ref[EXTRA_ROWS:, :] = summed.astype(BF16)


def join_kernel(slot_ref, *refs):
    amount = len(refs)
    groups = 0
    while 4 * groups + sum(refs[4 * i].shape[0] for i in range(groups)) < amount:
        groups += 1
    outs = refs[4 * groups :]
    index = 0
    for number in range(groups):
        blocks = refs[4 * number : 4 * number + 4]
        cols = blocks[0].shape[2]
        for item in range(blocks[0].shape[0]):
            for place in range(4):
                for slot in range(4):

                    @pl.when(slot_ref[place] == slot)
                    def _copy(index=index, item=item, slot=slot, place=place, blocks=blocks):
                        value = blocks[slot][item].astype(F32)
                        outs[index][:, place * cols : (place + 1) * cols] = value

            index += 1


def join(slots, *groups):
    return run(
        join_kernel,
        [
            ((group[0].shape[1], 4 * group[0].shape[2]), F32)
            for group in groups
            for _ in range(group[0].shape[0])
        ],
        *[block for group in groups for block in group],
        scalars=(slots,),
        vmem=32,
    )


def attn_join_kernel(out_cols, slot_ref, *refs):
    out_ref, query_ref, key_ref, value_ref, gain_ref, part_ref = refs[4:]
    for place in range(4):
        for slot in range(4):

            @pl.when(slot_ref[place] == slot)
            def _copy(slot=slot, place=place):
                part_ref[place] = refs[slot][...].astype(F32)

    parts = [part_ref[place, EXTRA_ROWS:, :] for place in range(4)]
    out_ref[...] = jnp.concatenate([part[:, :out_cols] for part in parts], axis=1).T
    lin = jnp.concatenate([part[:, out_cols:] for part in parts], axis=1)
    q_width = query_ref.shape[1]
    query_ref[...] = lin[:, :q_width]
    key_ref[...] = lin[:, q_width : q_width + HD].T
    value_ref[...] = lin[:, q_width + HD :].T
    gains = part_ref[0, :EXTRA_ROWS, :]
    for place in range(1, 4):
        gains = gains + part_ref[place, :EXTRA_ROWS, :]
    gain_ref[...] = gains


def per_device(
    rows,
    tokens,
    segment_ids,
    attn_gain,
    w_query,
    b_query,
    w_key,
    b_key,
    w_value,
    b_value,
    w_out,
    ffn_gain,
    w_gate,
    w_up,
    w_down,
    out_grad,
):
    count, width = tokens.shape
    half = count // 2
    d_rows = w_query.shape[0]
    q_width = w_query.shape[1]
    qk_width = q_width + HD
    lin_width = qk_width + HD
    heads = q_width // HD
    units = w_gate.shape[1] // 4
    row = lax.axis_index("row")
    group = lax.axis_index("dp")
    core = lax.axis_index("col")

    targets = [group, group ^ (1 + core), group ^ (2 - core), group ^ 3]
    slots = []
    for place in range(4):
        relative = group ^ place
        flipped = (relative & 1) * 2 + (relative >> 1)
        slots.append(jnp.where(core == 0, relative, flipped))
    slots = jnp.stack(slots).astype(jnp.int32)
    target_numbers = jnp.stack(targets).astype(jnp.int32)
    core_number = core[None].astype(jnp.int32)

    def row_send(value, step):
        return lax.ppermute(value, "row", [(i, (i + step) % rows) for i in range(rows)])

    row_number = row[None].astype(jnp.int32)

    def ring(value):
        return row_send(value, 1)

    def ring_add(moved, parts, step, *late):
        place = ((row + rows - step) % rows)[None].astype(jnp.int32)
        return run(
            ring_add_kernel,
            [(moved.shape, BF16)],
            moved,
            scalars=(place,),
            late=late,
            far=(parts,),
            scratch=[pltpu.VMEM(moved.shape, BF16), pltpu.SemaphoreType.DMA],
        )[0]

    gain_one = attn_gain.astype(F32)[None, :]
    gain_two = ffn_gain.astype(F32)[None, :]
    inputs = tokens.astype(F32)
    normed1 = (inputs * inverse_rms(inputs) * gain_one).astype(BF16)
    def own_half(values):
        return lax.dynamic_slice_in_dim(values, core * half, half, axis=0)

    with jax.named_scope("out_grad_gather"):
        grad_blocks = dp_gather(own_half(out_grad))
        grad_own = stacked(grad_blocks)
        grad_other = swap_core(grad_own)
    with jax.named_scope("attn_weights"):
        block = jnp.concatenate([w_out.T, w_query, w_key, w_value], axis=1)
        block_cols = block.shape[1] // 4
        own_quarter = lax.dynamic_slice_in_dim(block, group * block_cols, block_cols, axis=1)
        quarters = gather(own_quarter, "row", rows).reshape(width, block_cols)
        w_blocks = dp_gather_wide(stacked([quarters], *grad_blocks[1:]))[0]

    def split_gather(own, *late):
        own = stacked(dp_gather(own), *late)
        return (own, swap_core(own))

    def split_send(own, other):
        moved = swap_core(other)
        blocks = moved.reshape(4, half, width)
        own = own.reshape(4, half, width)
        parts = [own[place] + blocks[place].astype(F32) for place in range(4)]
        arrived = [dp_send(part.astype(BF16), step) for step, part in enumerate(parts[1:])]
        return (parts[0], arrived, moved)

    def split_sum(own, arrived, *late):
        done = run(sum_kernel, [((half, width), BF16)], own, *arrived, late=late)[0]
        return (done, swap_core(done))

    bias = jnp.concatenate([b_query, b_key, b_value]).astype(F32)[None, :]
    positions = (row * count + jnp.arange(count, dtype=jnp.int32)).astype(F32)
    ladder = (jnp.arange(2 * HD, dtype=jnp.int32) % HALF).astype(F32) * (2.0 / HD)
    angles = positions[:, None] * jnp.exp(-ladder * jnp.log(ROPE_BASE))[None, :]
    cos_table, sin_table = jnp.cos(angles), jnp.sin(angles)
    seg_rows = count // LANES
    seg_own = segment_ids.astype(BF16).reshape(seg_rows, LANES)
    seg_own = jnp.pad(seg_own, ((0, EXTRA_ROWS - seg_rows), (0, 0)))
    query_meta = jnp.stack([positions, segment_ids.astype(F32)], axis=1)
    with jax.named_scope("ffn_weights"):
        own_ffn = [
            lax.dynamic_slice_in_dim(weight, group * units, units, axis=1)
            for weight in (w_gate, w_up, w_down.T)
        ]
        part = ((3, d_rows, units), BF16)
        (own_ffn,) = run(parts_kernel, [part], *own_ffn, late=(quarters,))
        ffn_pieces = [own_ffn, ring(own_ffn)]
    with jax.named_scope("lin"):
        queries, kv_own, w_attn = run(
            lin_kernel,
            [
                ((count, q_width), BF16),
                ((count + EXTRA_ROWS, 2 * HD), BF16),
                ((width, 4 * block_cols), BF16),
            ],
            normed1, bias, cos_table, sin_table, seg_own, *w_blocks,
            scalars=(slots,),
            load=True,
            vmem=60,
        )
    with jax.named_scope("kv_move"):
        kv_all = [kv_own] + [
            lax.ppermute(kv_own, "row", [(i, i + step) for i in range(rows - step)])
            for step in range(1, rows)
        ]
    with jax.named_scope("ffn_weights"):
        ffn_pieces.append(ring(run(parts_kernel, [part], ffn_pieces[1], late=kv_all[1:])[0]))
    block = jnp.repeat(jnp.arange(rows, dtype=jnp.int32), count)
    within = jnp.tile(jnp.arange(count, dtype=jnp.int32), rows)
    key_pos = jnp.where(block <= row, (row - block) * count + within, 2**30)
    key_pos = jnp.broadcast_to(key_pos.astype(F32)[None, :], (8, rows * count))

    key_count = rows * count
    with jax.named_scope("attention"):
        attn_out, attn_heads, log_sum, branch = run(
            functools.partial(attend_kernel, heads),
            [
                ((count, q_width), F32),
                ((count, q_width), BF16),
                ((count, LANES), F32),
                ((count, width), BF16),
            ],
            queries, query_meta, key_pos, w_attn, *kv_all,
            scratch=[pltpu.VMEM((count, key_count), F32)],
            load=True,
            vmem=60,
        )
        residual, normed2 = run(
            norm_kernel,
            [((count, width), F32), ((half, width), BF16)],
            tokens, branch, swap_core(branch), gain_two,
            scalars=(core_number,),
            late=(grad_other,),
            scratch=[pltpu.VMEM((count, width), F32)],
        )

    with jax.named_scope("ffn_weights"):
        for _ in range(3, rows):
            onward = run(parts_kernel, [part], ffn_pieces[-1], late=(normed2,))[0]
            ffn_pieces.append(ring(onward))
    with jax.named_scope("normed2_gather"):
        normed_own, normed_other = split_gather(normed2, ffn_pieces[-1])
    with jax.named_scope("ffn_weights"):
        (ffn_w,) = run(
            place_kernel,
            [((rows, 3, d_rows, units), BF16)],
            *ffn_pieces,
            scalars=(row_number,),
            vmem=32,
        )
    amount = 4 * half
    wide = ((2, amount, units), BF16)
    ffn_outs = [((amount, width), F32), ((amount, width), BF16), wide, wide, wide]
    with jax.named_scope("ffn"):
        dn_own, dn_other, hidden, d_gate, d_up = run(
            ffn_kernel,
            ffn_outs,
            normed_own, normed_other, grad_own, grad_other, ffn_w,
            scratch=[pltpu.VMEM((width, units), BF16)] * 3,
            flops=13 * 10**9,
        )
    with jax.named_scope("d_normed2_sum"):
        dn_kept, dn_arrived, moved = split_send(dn_own, dn_other)
    with jax.named_scope("ffn_grads"):
        ffn_grads, first_grads = run(
            ffn_grad_kernel,
            [((rows, 3, d_rows, units), BF16), part],
            normed_own, normed_other, d_gate, normed_own, normed_other, d_up,
            grad_own, grad_other, hidden,
            scalars=(((row + rows - 1) % rows)[None].astype(jnp.int32),),
            late=(moved,),
            flops=13 * 10**9,
        )
    with jax.named_scope("ffn_grad_rows"):
        ring_sums = []

    with jax.named_scope("d_normed2_sum"):
        d_normed_own, d_normed_other = split_sum(dn_kept, dn_arrived, ffn_grads)

    def ring_stage(*late):
        if len(ring_sums) < rows - 1:
            moved_sum = ring_sums[-1] if ring_sums else first_grads
            step = len(ring_sums) + 2
            ring_sums.append(ring_add(ring(moved_sum), ffn_grads, step, *late))
        return ring_sums[-1]

    with jax.named_scope("ffn_grad_rows"):
        stage_one = ring_stage(d_normed_own)
    with jax.named_scope("attention_back"):
        d_residual, d_low, dq, d_gain_two, *dkv_parts = run(
            functools.partial(back_kernel, heads),
            [
                ((count, width), F32),
                ((count, width), BF16),
                ((count, q_width), BF16),
                ((8, width), F32),
            ]
            + [((count, 2 * HD), BF16)] * rows,
            d_normed_own, d_normed_other, residual, out_grad, gain_two, w_attn, cos_table,
            sin_table, queries, query_meta, key_pos, attn_out, log_sum, *kv_all,
            scalars=(core_number,),
            scratch=[pltpu.VMEM((count, width), F32), pltpu.VMEM((count, key_count), F32)],
            late=(stage_one,),
            load=True,
            vmem=60,
        )
    with jax.named_scope("out_grads"):
        out_cols = q_width // 4
        (out_parts,) = run(
            out_grad_kernel, [((4, out_cols, width), BF16)], attn_heads, d_low
        )
        out_moved = exchange(out_parts, "dp")
    with jax.named_scope("dkv_move"):
        dkv = [dkv_parts[0]] + [
            lax.ppermute(dkv_parts[step], "row", [(i + step, i) for i in range(rows - step)])
            for step in range(1, rows)
        ]
    with jax.named_scope("ffn_grad_rows"):
        stage_two = ring_stage(*dkv[1:])
    with jax.named_scope("d_lin"):
        lin_cols = lin_width // 4
        d_normed1, bias_sum, *lin_blocks = run(
            lin_back_kernel,
            [
                ((count, width), BF16),
                ((8, lin_width), F32),
                ((lin_cols, width), F32),
            ]
            + [((lin_cols, width), BF16)] * 3,
            dq, cos_table, sin_table, w_attn, normed1, *dkv,
            scalars=(target_numbers,),
            late=(stage_two, out_moved),
            scratch=[pltpu.VMEM((lin_width, width), F32)],
            load=True,
            vmem=60,
        )
    with jax.named_scope("lin_grads"):
        lin_moved = [lin_blocks[0]] + [
            dp_send(lin_blocks[step + 1], step) for step in range(3)
        ]
    with jax.named_scope("d_normed1"):
        grad_tokens, d_gain_one = run(
            final_kernel,
            [((count, width), BF16), ((8, width), F32)],
            tokens, d_normed1, swap_core(d_normed1), gain_one, d_residual,
        )
    pack_width = out_cols + lin_cols
    packet = ((EXTRA_ROWS + d_rows, pack_width), BF16)
    with jax.named_scope("ffn_grad_rows"):
        stage_three = ring_stage(*lin_moved[1:])
        while len(ring_sums) < rows - 1:
            stage_three = ring_stage()
    with jax.named_scope("ffn_grad_groups"):
        flat = stage_three.reshape(3 * d_rows, units)
        ffn_done, passed = dp_gather_wide(flat)
        ffn_done = [block.reshape(3, d_rows, units) for block in ffn_done]
    with jax.named_scope("attn_grads"):
        packets = run(
            packet_kernel,
            [packet] * rows,
            d_gain_one, d_gain_two, bias_sum, out_moved, *lin_moved,
            scalars=(row_number,),
            late=(stage_three,),
            scratch=[pltpu.VMEM((width, pack_width), F32)],
        )
    with jax.named_scope("ffn_branch_sum"):
        branch_own, branch_other = run(
            ffn_out_kernel,
            [((amount, width), F32), ((amount, width), BF16)],
            hidden, ffn_w,
            late=(stage_three,),
            scratch=[pltpu.VMEM((width, units), BF16)],
        )
        (branch_parts,) = run(
            core_sum_kernel,
            [((4, half, width), BF16)],
            branch_own, swap_core(branch_other),
            scalars=(target_numbers,),
        )
        branch_moved = exchange(branch_parts, "dp")
        (own,) = run(sum_four_kernel, [((half, width), BF16)], branch_moved)
        other = swap_core(own)
        low = jnp.where(core == 0, own, other).astype(F32)
        high = jnp.where(core == 0, other, own).astype(F32)
        output = (residual + jnp.concatenate([low, high], axis=0)).astype(BF16)
    with jax.named_scope("attn_grad_rows"):
        packets = [packets[0]] + [row_send(packets[step], step) for step in range(1, rows)]
    with jax.named_scope("attn_grad_rows"):
        (attn_sum,) = run(
            packet_sum_kernel,
            [packet],
            *packets,
            scalars=(row_number,),
            scratch=[pltpu.VMEM((rows, EXTRA_ROWS, pack_width), F32)],
        )
    with jax.named_scope("attn_grad_groups"):
        attn_done = dp_gather(attn_sum)
    with jax.named_scope("joins"):
        grad_w_gate, grad_w_up, grad_w_down_t = join(slots, ffn_done)
        grad_w_out, grad_w_query, grad_w_key, grad_w_value, smalls = run(
            functools.partial(attn_join_kernel, out_cols),
            [
                ((q_width, d_rows), F32),
                ((d_rows, q_width), F32),
                ((HD, d_rows), F32),
                ((HD, d_rows), F32),
                ((EXTRA_ROWS, pack_width), F32),
            ],
            *attn_done,
            scalars=(slots,),
            late=passed,
            scratch=[pltpu.VMEM((4, EXTRA_ROWS + d_rows, pack_width), F32)],
        )
    lines = -(-width // pack_width)
    gain_rows = [smalls[at : at + lines].reshape(-1)[:width] for at in (0, lines)]
    biases = smalls[2 * lines :].reshape(-1)[:lin_width]
    return (
        output,
        grad_tokens,
        gain_rows[0],
        grad_w_query,
        biases[:q_width],
        grad_w_key.T,
        biases[q_width:qk_width],
        grad_w_value.T,
        biases[qk_width:],
        grad_w_out,
        gain_rows[1],
        grad_w_gate,
        grad_w_up,
        grad_w_down_t.T,
    )


def solution(mesh):
    return jax.shard_map(
        functools.partial(per_device, mesh.shape["row"]),
        mesh=mesh,
        in_specs=(
            P(("dp", "row"), None),
            P(("dp", "row")),
            P(),
            P("row", "col"),
            P("col"),
            P("row", "col"),
            P("col"),
            P("row", "col"),
            P("col"),
            P("col", "row"),
            P(),
            P("row", "col"),
            P("row", "col"),
            P("col", "row"),
            P(("dp", "row"), None),
        ),
        out_specs=(
            P(("dp", "row"), None),
            P(("dp", "row"), None),
            P(),
            P("row", "col"),
            P("col"),
            P("row", "col"),
            P("col"),
            P("row", "col"),
            P("col"),
            P("col", "row"),
            P(),
            P("row", "col"),
            P("row", "col"),
            P("col", "row"),
        ),
        check_vma=False,
    )
```

```python
import functools

import jax
import jax.numpy as jnp
from jax import lax
from jax.experimental import pallas as pl
from jax.experimental.pallas import tpu as pltpu
from jax.sharding import PartitionSpec as P

HD = 64
HALF = HD // 2
NORM_EPS = 1e-06
ROPE_BASE = 1000000.0
NEG_BIG = -1e30
LANES = 128
EXTRA_ROWS = 16
BF16 = jnp.bfloat16
F32 = jnp.float32


def dot_rows(left, right):
    return lax.dot_general(left, right, (((0,), (0,)), ((), ())), preferred_element_type=F32)


def dot_cols(left, right):
    return lax.dot_general(left, right, (((1,), (1,)), ((), ())), preferred_element_type=F32)


def dot(left, right):
    return jnp.dot(left, right, preferred_element_type=F32)


def inverse_rms(values):
    return lax.rsqrt(jnp.mean(values * values, axis=1, keepdims=True) + NORM_EPS)


def norm_back(gradient, unit_rows, inv_rms, gain):
    scaled = gradient * gain
    inner = jnp.mean(scaled * unit_rows, axis=1, keepdims=True)
    return (inv_rms * (scaled - unit_rows * inner), jnp.sum(gradient * unit_rows, axis=0))


def after(value, *others):
    for other in others:
        first = other[(0,) * other.ndim].astype(F32)
        value = value + jnp.minimum(jnp.abs(first), 0.0).astype(value.dtype)
    return value


def swap_core(value):
    return lax.ppermute(value, "col", [(0, 1), (1, 0)])


def exchange(parts, axis):
    return lax.all_to_all(parts, axis, split_axis=0, concat_axis=0, tiled=True)


def gather(value, axis, size):
    return exchange(jnp.broadcast_to(value[None], (size,) + value.shape), axis)


def dp_send(value, step):
    pairs = []
    for group in range(4):
        for core in range(2):
            bits = 3 if step == 2 else 1 << ((step + core) % 2)
            pairs.append((group * 2 + core, (group ^ bits) * 2 + core))
    return lax.ppermute(value, ("dp", "col"), pairs)


def dp_gather(value):
    return [value] + [dp_send(value, step) for step in range(3)]


def dp_gather_wide(value):
    first, second = dp_send(value, 0), dp_send(value, 1)
    half = value.shape[0] // 2
    passed = (first[:half], second[half:])
    far = jnp.concatenate([dp_send(passed[0], 1), dp_send(passed[1], 0)], axis=0)
    return ([value, first, second, far], passed)


def dp_scatter_sum(parts):
    moved = [dp_send(part.astype(BF16), step) for step, part in enumerate(parts[1:])]
    return parts[0] + moved[0].astype(F32) + moved[1].astype(F32) + moved[2].astype(F32)


def pick(stacked, place):
    return lax.dynamic_index_in_dim(stacked, place, axis=0, keepdims=False)


def sum_parts(parts):
    return jnp.sum(parts.astype(F32), axis=0)


def half_turn(values):
    width = values.shape[1]
    lane = lax.broadcasted_iota(jnp.int32, values.shape, 1) % HD
    return jnp.where(
        lane < HALF, -pltpu.roll(values, width - HALF, 1), pltpu.roll(values, HALF, 1)
    )


def turned(values, cos, sin):
    copies = values.shape[1] // cos.shape[1]
    cos = jnp.concatenate([cos] * copies, axis=1)
    sin = jnp.concatenate([sin] * copies, axis=1)
    return values * cos + half_turn(values) * sin


def run(
    kernel, outs, *operands, scalars=(), late=(), far=(), scratch=(), flops=1, load=False, vmem=48
):
    leads = len(scalars) + len(late)
    first = leads + len(far)
    amount = len(operands)
    spec = pl.BlockSpec(memory_space=pltpu.VMEM)
    anywhere = pl.BlockSpec(memory_space=pl.ANY)

    def body(*refs):
        held, rest = refs[first : first + amount], refs[first + amount :]
        if load:
            sources, held, sems = held, rest[len(rest) - amount - 1 : -1], rest[-1]
            rest = rest[: len(rest) - amount - 1]
            copies = [
                pltpu.make_async_copy(source, place, sems.at[number])
                for number, (source, place) in enumerate(zip(sources, held))
            ]
            for copy in copies:
                copy.start()
            for copy in copies:
                copy.wait()
        kernel(*refs[: len(scalars)], *refs[leads:first], *held, *rest)

    places = [pltpu.VMEM(operand.shape, operand.dtype) for operand in operands] if load else []
    return pl.pallas_call(
        body,
        out_shape=tuple(jax.ShapeDtypeStruct(shape, dtype) for shape, dtype in outs),
        in_specs=[pl.BlockSpec(memory_space=pltpu.SMEM)] * len(scalars)
        + [anywhere] * (len(late) + len(far))
        + [anywhere if load else spec] * amount,
        out_specs=tuple([spec] * len(outs)),
        scratch_shapes=list(scratch)
        + places
        + ([pltpu.SemaphoreType.DMA((amount,))] if load else []),
        compiler_params=pltpu.CompilerParams(vmem_limit_bytes=vmem * 2**20),
        cost_estimate=pl.CostEstimate(flops=flops, bytes_accessed=2**20, transcendentals=0),
    )(*scalars, *late, *far, *operands)


def copy_kernel(*refs):
    out_ref = refs[-1]
    begin = 0
    for ref in refs[:-1]:
        out_ref[begin : begin + ref.shape[0], :] = ref[...]
        begin += ref.shape[0]


def stacked(blocks, *late):
    amount = sum(block.shape[0] for block in blocks)
    return run(
        copy_kernel, [((amount, blocks[0].shape[1]), blocks[0].dtype)], *blocks, late=late, vmem=32
    )[0]


def parts_kernel(*refs):
    out_ref = refs[-1]
    if len(refs) == 2:
        out_ref[...] = refs[0][...]
    else:
        for part, ref in enumerate(refs[:-1]):
            out_ref[part] = ref[...]


def place_kernel(row_ref, *refs):
    out_ref = refs[-1]
    rows = len(refs) - 1
    for step in range(rows):
        out_ref[(row_ref[0] + rows - step) % rows] = refs[step][...]


def sum_kernel(own_ref, first_ref, second_ref, both_ref, out_ref):
    summed = own_ref[...] + first_ref[...].astype(F32) + second_ref[...].astype(F32)
    out_ref[...] = (summed + both_ref[...].astype(F32)).astype(BF16)


def core_sum_kernel(target_ref, own_ref, moved_ref, out_ref):
    half = out_ref.shape[1]
    for place in range(4):
        part = slice(place * half, (place + 1) * half)
        summed = own_ref[part, :] + moved_ref[part, :].astype(F32)
        out_ref[target_ref[place]] = summed.astype(BF16)


def sum_four_kernel(parts_ref, out_ref):
    summed = parts_ref[0].astype(F32)
    for place in range(1, 4):
        summed = summed + parts_ref[place].astype(F32)
    out_ref[...] = summed.astype(BF16)


def ring_add_kernel(place_ref, parts_ref, moved_ref, out_ref, block_ref, sem):
    copy = pltpu.make_async_copy(parts_ref.at[place_ref[0]], block_ref, sem)
    copy.start()
    copy.wait()
    out_ref[...] = (moved_ref[...].astype(F32) + block_ref[...].astype(F32)).astype(BF16)


def lin_kernel(
    slot_ref, n_ref, bias_ref, cos_ref, sin_ref, seg_ref, *refs
):
    q_ref, kv_ref, w_ref = refs[4:]
    count = n_ref.shape[0]
    q_width = q_ref.shape[1]
    cols = refs[0].shape[1]
    for place in range(4):
        for slot in range(4):

            @pl.when(slot_ref[place] == slot)
            def _copy(slot=slot, place=place):
                w_ref[:, place * cols : (place + 1) * cols] = refs[slot][...]

    lin = dot(n_ref[...], w_ref[...])[:, q_width:] + bias_ref[...]
    rot = turned(lin[:, : q_width + HD], cos_ref[...], sin_ref[...])
    q_ref[...] = (rot[:, :q_width].astype(BF16).astype(F32) * HD ** (-0.5)).astype(BF16)
    kv = jnp.concatenate([rot[:, q_width:], lin[:, q_width + HD :]], axis=1)
    kv_ref[:count, :] = kv.astype(BF16)
    kv_ref[count:, :] = seg_ref[...]


def read_keys(kv_refs, meta_ref, pos_ref, bias_ref):
    count = kv_refs[0].shape[0] - EXTRA_ROWS
    joined_rows = jnp.concatenate([ref[:count, :] for ref in kv_refs], axis=0)
    docs = []
    for ref in kv_refs:
        extra = ref[count:, :].astype(F32)
        docs += [extra[line : line + 1, :] for line in range(count // LANES)]
    key_doc = jnp.concatenate(docs, axis=1)
    allowed = (pos_ref[0:1, :] <= meta_ref[:, 0:1]) & (key_doc == meta_ref[:, 1:2])
    bias_ref[...] = jnp.where(allowed, 0.0, NEG_BIG)
    return (joined_rows[:, :HD], joined_rows[:, HD:])


def attend_kernel(heads, q_ref, meta_ref, pos_ref, w_ref, *refs):
    out_ref, low_ref, lse_ref, branch_ref, bias_ref = refs[-5:]
    keys, values = read_keys(refs[:-5], meta_ref, pos_ref, bias_ref)
    lane = lax.broadcasted_iota(jnp.int32, lse_ref.shape, 1)
    lse_all = jnp.zeros(lse_ref.shape, F32)
    outs = []
    for head in range(heads):
        cols = slice(head * HD, (head + 1) * HD)
        scores = dot_cols(q_ref[:, cols], keys) + bias_ref[...]
        top = jnp.max(scores, axis=1, keepdims=True)
        weights = jnp.exp(scores - top)
        total = jnp.sum(weights, axis=1, keepdims=True)
        outs.append(dot(weights.astype(BF16), values) / total)
        lse_all = jnp.where(lane == head, top + jnp.log(total), lse_all)
    heads_sum = jnp.concatenate(outs, axis=1)
    low = heads_sum.astype(BF16)
    out_ref[...] = heads_sum
    low_ref[...] = low
    lse_ref[...] = lse_all
    branch_ref[...] = dot_cols(low, w_ref[:, : heads * HD]).astype(BF16)


def norm_kernel(core_ref, x_ref, own_ref, other_ref, gain_ref, res_ref, half_ref, norm_ref):
    half = half_ref.shape[0]
    residual = x_ref[...].astype(F32) + (own_ref[...].astype(F32) + other_ref[...].astype(F32))
    res_ref[...] = residual
    norm_ref[...] = residual * inverse_rms(residual) * gain_ref[...]
    start = pl.multiple_of(core_ref[0] * half, half)
    half_ref[...] = norm_ref[pl.ds(start, half), :].astype(BF16)


def ffn_kernel(
    n_own, n_other, g_own, g_other, w_ref,
    dn_own, dn_other, hidden_ref, dgate_ref, dup_ref, gate_ref, up_ref, down_ref,
):
    size = w_ref.shape[2]
    for place in range(w_ref.shape[0]):
        for part, ref in enumerate((gate_ref, up_ref, down_ref)):
            ref[place * size : (place + 1) * size, :] = w_ref[place, part]
    ffn_math(
        n_own, n_other, g_own, g_other, gate_ref, up_ref, down_ref,
        dn_own, dn_other, hidden_ref, dgate_ref, dup_ref,
    )


def ffn_math(
    n_own, n_other, g_own, g_other, gate_ref, up_ref, down_ref,
    dn_own, dn_other, hidden_ref, dgate_ref, dup_ref,
):
    amount = n_own.shape[0]
    tile = min(256, amount)
    for side, n_ref, g_ref in ((1, n_other, g_other), (0, n_own, g_own)):
        for begin in range(0, amount, tile):
            part = slice(begin, begin + tile)
            normed = n_ref[part, :]
            gate = dot(normed, gate_ref[...])
            up = dot(normed, up_ref[...])
            d_hidden = dot(g_ref[part, :], down_ref[...])
            sig = 1.0 / (1.0 + jnp.exp(-gate))
            silu = gate * sig
            hidden_ref[side, part, :] = (silu * up).astype(BF16)
            d_gate = (d_hidden * up * sig * (1.0 + gate * (1.0 - sig))).astype(BF16)
            d_up = (d_hidden * silu).astype(BF16)
            dgate_ref[side, part, :] = d_gate
            dup_ref[side, part, :] = d_up
            d_normed = dot_cols(d_gate, gate_ref[...]) + dot_cols(d_up, up_ref[...])
            if side == 1:
                dn_other[part, :] = d_normed.astype(BF16)
            else:
                dn_own[part, :] = d_normed


def ffn_grad_kernel(first_ref, *refs):
    out_ref, begin_ref = refs[-2:]
    size = out_ref.shape[2]
    for item in range(out_ref.shape[1]):
        own, other, right = refs[3 * item : 3 * item + 3]
        summed = dot_rows(own[...], right[0]) + dot_rows(other[...], right[1])
        for place in range(out_ref.shape[0]):
            out_ref[place, item] = summed[place * size : (place + 1) * size].astype(BF16)
    begin_ref[...] = out_ref[first_ref[0]]


def out_grad_kernel(heads_ref, low_ref, out_ref):
    cols = out_ref.shape[1]
    product = dot_rows(heads_ref[...], low_ref[...])
    for place in range(4):
        out_ref[place] = product[place * cols : (place + 1) * cols].astype(BF16)


def ffn_out_kernel(hidden_ref, w_ref, own_ref, other_ref, down_ref):
    size = w_ref.shape[2]
    for place in range(w_ref.shape[0]):
        down_ref[place * size : (place + 1) * size, :] = w_ref[place, 2]
    other_ref[...] = dot_cols(hidden_ref[1], down_ref[...]).astype(BF16)
    own_ref[...] = dot_cols(hidden_ref[0], down_ref[...])


def back_kernel(
    heads, core_ref, dn_own, dn_other, res_ref, grad_ref, gain_ref, w_ref, cos_ref, sin_ref,
    q_ref, meta_ref, pos_ref, out_ref, lse_ref, *refs,
):
    rows = (len(refs) - 6) // 2
    dres_ref, dlow_ref, dq_ref, dgain_ref = refs[rows : rows + 4]
    dkv_refs = refs[rows + 4 : 2 * rows + 4]
    dn_ref, bias_ref = refs[-2:]
    half = dn_own.shape[0]
    core = core_ref[0]
    dn_ref[pl.ds(pl.multiple_of(core * half, half), half), :] = dn_own[...].astype(F32)
    dn_ref[pl.ds(pl.multiple_of((1 - core) * half, half), half), :] = dn_other[...].astype(F32)
    d_normed = dn_ref[...]
    residual = res_ref[...]
    inv = inverse_rms(residual)
    unit = residual * inv
    d_norm, d_gain = norm_back(d_normed, unit, inv, gain_ref[...])
    dgain_ref[...] = jnp.broadcast_to(d_gain[None, :], dgain_ref.shape)
    d_res = grad_ref[...].astype(F32) + d_norm
    dres_ref[...] = d_res
    d_low = d_res.astype(BF16)
    dlow_ref[...] = d_low
    d_heads = dot(d_low, w_ref[:, : heads * HD]).astype(BF16)
    keys, values = read_keys(refs[:rows], meta_ref, pos_ref, bias_ref)
    d_keys = jnp.zeros(keys.shape, F32)
    d_values = jnp.zeros(keys.shape, F32)
    dqs = []
    for head in range(heads):
        cols = slice(head * HD, (head + 1) * HD)
        queries = q_ref[:, cols]
        grads = d_heads[:, cols]
        delta = jnp.sum(grads.astype(F32) * out_ref[:, cols], axis=1, keepdims=True)
        scores = dot_cols(queries, keys) + bias_ref[...]
        probs = jnp.exp(scores - lse_ref[:, head : head + 1])
        d_probs = dot_cols(grads, values)
        d_scores = (probs * (d_probs - delta)).astype(BF16)
        dqs.append(dot(d_scores, keys) * HD ** (-0.5))
        d_keys = d_keys + dot_rows(d_scores, queries)
        d_values = d_values + dot_rows(probs.astype(BF16), grads)
    dqs.append(jnp.zeros_like(dqs[0]))
    dq = turned(jnp.concatenate(dqs, axis=1), cos_ref[...], -sin_ref[...])
    dq_ref[...] = dq[:, : heads * HD].astype(BF16)
    dkv = jnp.concatenate([d_keys, d_values], axis=1).astype(BF16)
    count = dkv_refs[0].shape[0]
    for place, ref in enumerate(dkv_refs):
        ref[...] = dkv[place * count : (place + 1) * count]


def lin_back_kernel(target_ref, dq_ref, cos_ref, sin_ref, w_ref, n_ref, *refs):
    dn_ref, bias_ref = refs[-7:-5]
    blocks, product_ref = refs[-5:-1], refs[-1]
    dkv = refs[0][...].astype(F32)
    for ref in refs[1:-7]:
        dkv = dkv + ref[...].astype(F32)
    d_key = turned(dkv, cos_ref[...], -sin_ref[...])
    d_lin = jnp.concatenate(
        [dq_ref[...], d_key[:, :HD].astype(BF16), dkv[:, HD:].astype(BF16)], axis=1
    )
    product_ref[...] = dot_rows(d_lin, n_ref[...])
    cols = blocks[0].shape[0]
    for place, ref in enumerate(blocks):
        begin = pl.multiple_of(target_ref[place] * cols, cols)
        ref[...] = product_ref[pl.ds(begin, cols), :].astype(ref.dtype)
    nothing = jnp.zeros(dq_ref.shape, BF16)
    dn_ref[...] = dot_cols(jnp.concatenate([nothing, d_lin], axis=1), w_ref[...]).astype(BF16)
    bias = jnp.sum(d_lin.astype(F32), axis=0, keepdims=True)
    bias_ref[...] = jnp.broadcast_to(bias, bias_ref.shape)


def final_kernel(x_ref, own_ref, other_ref, gain_ref, dres_ref, grad_ref, dgain_ref):
    d_normed = own_ref[...].astype(F32) + other_ref[...].astype(F32)
    values = x_ref[...].astype(F32)
    inv = inverse_rms(values)
    d_norm, d_gain = norm_back(d_normed, values * inv, inv, gain_ref[...])
    grad_ref[...] = (dres_ref[...] + d_norm).astype(BF16)
    dgain_ref[...] = jnp.broadcast_to(d_gain[None, :], dgain_ref.shape)


def packet_kernel(row_ref, gain_one, gain_two, bias_ref, *refs):
    pack_ref = refs[-1]
    packets = refs[5:-1]
    out_ref = refs[0]
    out_sum = out_ref[0].astype(F32)
    for place in range(1, 4):
        out_sum = out_sum + out_ref[place].astype(F32)
    lin_sum = refs[1][...]
    for ref in refs[2:5]:
        lin_sum = lin_sum + ref[...].astype(F32)
    pack_ref[...] = jnp.concatenate([out_sum, lin_sum], axis=0).T
    cols = pack_ref.shape[1]
    lines = []
    for ref in (gain_one, gain_two, bias_ref):
        values = ref[0:1, :]
        spare = -values.shape[1] % cols
        values = jnp.concatenate([values, jnp.zeros((1, spare), F32)], axis=1)
        lines += [values[:, at : at + cols] for at in range(0, values.shape[1], cols)]
    lines.append(jnp.zeros((EXTRA_ROWS - len(lines), cols), F32))
    small = jnp.concatenate(lines, axis=0).astype(BF16)
    rows = len(packets)
    size = pack_ref.shape[0] // rows
    for step, packet in enumerate(packets):
        begin = pl.multiple_of(((row_ref[0] + step) % rows) * size, size)
        packet[:EXTRA_ROWS, :] = small
        packet[EXTRA_ROWS:, :] = pack_ref[pl.ds(begin, size), :].astype(BF16)


def packet_sum_kernel(row_ref, *refs):
    rows = len(refs) - 2
    out_ref, small_ref = refs[-2:]
    summed = refs[0][EXTRA_ROWS:, :].astype(F32)
    for ref in refs[1:rows]:
        summed = summed + ref[EXTRA_ROWS:, :].astype(F32)
    for step in range(rows):
        small_ref[(row_ref[0] + rows - step) % rows] = refs[step][:EXTRA_ROWS, :].astype(F32)
    small = small_ref[0]
    for place in range(1, rows):
        small = small + small_ref[place]
    out_ref[:EXTRA_ROWS, :] = small.astype(BF16)
    out_ref[EXTRA_ROWS:, :] = summed.astype(BF16)


def join_kernel(slot_ref, *refs):
    amount = len(refs)
    groups = 0
    while 4 * groups + sum(refs[4 * i].shape[0] for i in range(groups)) < amount:
        groups += 1
    outs = refs[4 * groups :]
    index = 0
    for number in range(groups):
        blocks = refs[4 * number : 4 * number + 4]
        cols = blocks[0].shape[2]
        for item in range(blocks[0].shape[0]):
            for place in range(4):
                for slot in range(4):

                    @pl.when(slot_ref[place] == slot)
                    def _copy(index=index, item=item, slot=slot, place=place, blocks=blocks):
                        value = blocks[slot][item].astype(F32)
                        outs[index][:, place * cols : (place + 1) * cols] = value

            index += 1


def join(slots, *groups):
    return run(
        join_kernel,
        [
            ((group[0].shape[1], 4 * group[0].shape[2]), F32)
            for group in groups
            for _ in range(group[0].shape[0])
        ],
        *[block for group in groups for block in group],
        scalars=(slots,),
        vmem=32,
    )


def attn_join_kernel(out_cols, slot_ref, *refs):
    out_ref, query_ref, key_ref, value_ref, gain_ref, part_ref = refs[4:]
    for place in range(4):
        for slot in range(4):

            @pl.when(slot_ref[place] == slot)
            def _copy(slot=slot, place=place):
                part_ref[place] = refs[slot][...].astype(F32)

    parts = [part_ref[place, EXTRA_ROWS:, :] for place in range(4)]
    out_ref[...] = jnp.concatenate([part[:, :out_cols] for part in parts], axis=1).T
    lin = jnp.concatenate([part[:, out_cols:] for part in parts], axis=1)
    q_width = query_ref.shape[1]
    query_ref[...] = lin[:, :q_width]
    key_ref[...] = lin[:, q_width : q_width + HD].T
    value_ref[...] = lin[:, q_width + HD :].T
    gains = part_ref[0, :EXTRA_ROWS, :]
    for place in range(1, 4):
        gains = gains + part_ref[place, :EXTRA_ROWS, :]
    gain_ref[...] = gains


def per_device(
    rows,
    tokens,
    segment_ids,
    attn_gain,
    w_query,
    b_query,
    w_key,
    b_key,
    w_value,
    b_value,
    w_out,
    ffn_gain,
    w_gate,
    w_up,
    w_down,
    out_grad,
):
    count, width = tokens.shape
    half = count // 2
    d_rows = w_query.shape[0]
    q_width = w_query.shape[1]
    qk_width = q_width + HD
    lin_width = qk_width + HD
    heads = q_width // HD
    units = w_gate.shape[1] // 4
    row = lax.axis_index("row")
    group = lax.axis_index("dp")
    core = lax.axis_index("col")

    targets = [group, group ^ (1 + core), group ^ (2 - core), group ^ 3]
    slots = []
    for place in range(4):
        relative = group ^ place
        flipped = (relative & 1) * 2 + (relative >> 1)
        slots.append(jnp.where(core == 0, relative, flipped))
    slots = jnp.stack(slots).astype(jnp.int32)
    target_numbers = jnp.stack(targets).astype(jnp.int32)
    core_number = core[None].astype(jnp.int32)

    def row_send(value, step):
        return lax.ppermute(value, "row", [(i, (i + step) % rows) for i in range(rows)])

    row_number = row[None].astype(jnp.int32)

    def ring(value):
        return row_send(value, 1)

    def ring_add(moved, parts, step, *late):
        place = ((row + rows - step) % rows)[None].astype(jnp.int32)
        return run(
            ring_add_kernel,
            [(moved.shape, BF16)],
            moved,
            scalars=(place,),
            late=late,
            far=(parts,),
            scratch=[pltpu.VMEM(moved.shape, BF16), pltpu.SemaphoreType.DMA],
        )[0]

    gain_one = attn_gain.astype(F32)[None, :]
    gain_two = ffn_gain.astype(F32)[None, :]
    inputs = tokens.astype(F32)
    normed1 = (inputs * inverse_rms(inputs) * gain_one).astype(BF16)
    def own_half(values):
        return lax.dynamic_slice_in_dim(values, core * half, half, axis=0)

    with jax.named_scope("out_grad_gather"):
        grad_blocks = dp_gather(own_half(out_grad))
        grad_own = stacked(grad_blocks)
        grad_other = swap_core(grad_own)
    with jax.named_scope("attn_weights"):
        block = jnp.concatenate([w_out.T, w_query, w_key, w_value], axis=1)
        block_cols = block.shape[1] // 4
        own_quarter = lax.dynamic_slice_in_dim(block, group * block_cols, block_cols, axis=1)
        quarters = gather(own_quarter, "row", rows).reshape(width, block_cols)
        w_blocks = dp_gather_wide(stacked([quarters], *grad_blocks[1:]))[0]

    def split_gather(own, *late):
        own = stacked(dp_gather(own), *late)
        return (own, swap_core(own))

    def split_send(own, other):
        moved = swap_core(other)
        blocks = moved.reshape(4, half, width)
        own = own.reshape(4, half, width)
        parts = [own[place] + blocks[place].astype(F32) for place in range(4)]
        arrived = [dp_send(part.astype(BF16), step) for step, part in enumerate(parts[1:])]
        return (parts[0], arrived, moved)

    def split_sum(own, arrived, *late):
        done = run(sum_kernel, [((half, width), BF16)], own, *arrived, late=late)[0]
        return (done, swap_core(done))

    bias = jnp.concatenate([b_query, b_key, b_value]).astype(F32)[None, :]
    positions = (row * count + jnp.arange(count, dtype=jnp.int32)).astype(F32)
    ladder = (jnp.arange(2 * HD, dtype=jnp.int32) % HALF).astype(F32) * (2.0 / HD)
    angles = positions[:, None] * jnp.exp(-ladder * jnp.log(ROPE_BASE))[None, :]
    cos_table, sin_table = jnp.cos(angles), jnp.sin(angles)
    seg_rows = count // LANES
    seg_own = segment_ids.astype(BF16).reshape(seg_rows, LANES)
    seg_own = jnp.pad(seg_own, ((0, EXTRA_ROWS - seg_rows), (0, 0)))
    query_meta = jnp.stack([positions, segment_ids.astype(F32)], axis=1)
    with jax.named_scope("ffn_weights"):
        own_ffn = [
            lax.dynamic_slice_in_dim(weight, group * units, units, axis=1)
            for weight in (w_gate, w_up, w_down.T)
        ]
        part = ((3, d_rows, units), BF16)
        (own_ffn,) = run(parts_kernel, [part], *own_ffn, late=(quarters,))
        ffn_pieces = [own_ffn, ring(own_ffn)]
    with jax.named_scope("lin"):
        queries, kv_own, w_attn = run(
            lin_kernel,
            [
                ((count, q_width), BF16),
                ((count + EXTRA_ROWS, 2 * HD), BF16),
                ((width, 4 * block_cols), BF16),
            ],
            normed1, bias, cos_table, sin_table, seg_own, *w_blocks,
            scalars=(slots,),
            load=True,
            vmem=60,
        )
    with jax.named_scope("kv_move"):
        kv_all = [kv_own] + [
            lax.ppermute(kv_own, "row", [(i, i + step) for i in range(rows - step)])
            for step in range(1, rows)
        ]
    with jax.named_scope("ffn_weights"):
        ffn_pieces.append(ring(run(parts_kernel, [part], ffn_pieces[1], late=kv_all[1:])[0]))
    block = jnp.repeat(jnp.arange(rows, dtype=jnp.int32), count)
    within = jnp.tile(jnp.arange(count, dtype=jnp.int32), rows)
    key_pos = jnp.where(block <= row, (row - block) * count + within, 2**30)
    key_pos = jnp.broadcast_to(key_pos.astype(F32)[None, :], (8, rows * count))

    key_count = rows * count
    with jax.named_scope("attention"):
        attn_out, attn_heads, log_sum, branch = run(
            functools.partial(attend_kernel, heads),
            [
                ((count, q_width), F32),
                ((count, q_width), BF16),
                ((count, LANES), F32),
                ((count, width), BF16),
            ],
            queries, query_meta, key_pos, w_attn, *kv_all,
            scratch=[pltpu.VMEM((count, key_count), F32)],
            load=True,
            vmem=60,
        )
        residual, normed2 = run(
            norm_kernel,
            [((count, width), F32), ((half, width), BF16)],
            tokens, branch, swap_core(branch), gain_two,
            scalars=(core_number,),
            late=(grad_other,),
            scratch=[pltpu.VMEM((count, width), F32)],
        )

    with jax.named_scope("ffn_weights"):
        for _ in range(3, rows):
            onward = run(parts_kernel, [part], ffn_pieces[-1], late=(normed2,))[0]
            ffn_pieces.append(ring(onward))
    with jax.named_scope("normed2_gather"):
        normed_own, normed_other = split_gather(normed2, ffn_pieces[-1])
    with jax.named_scope("ffn_weights"):
        (ffn_w,) = run(
            place_kernel,
            [((rows, 3, d_rows, units), BF16)],
            *ffn_pieces,
            scalars=(row_number,),
            vmem=32,
        )
    amount = 4 * half
    wide = ((2, amount, units), BF16)
    ffn_outs = [((amount, width), F32), ((amount, width), BF16), wide, wide, wide]
    with jax.named_scope("ffn"):
        dn_own, dn_other, hidden, d_gate, d_up = run(
            ffn_kernel,
            ffn_outs,
            normed_own, normed_other, grad_own, grad_other, ffn_w,
            scratch=[pltpu.VMEM((width, units), BF16)] * 3,
            flops=13 * 10**9,
        )
    with jax.named_scope("d_normed2_sum"):
        dn_kept, dn_arrived, moved = split_send(dn_own, dn_other)
    with jax.named_scope("ffn_grads"):
        ffn_grads, first_grads = run(
            ffn_grad_kernel,
            [((rows, 3, d_rows, units), BF16), part],
            normed_own, normed_other, d_gate, normed_own, normed_other, d_up,
            grad_own, grad_other, hidden,
            scalars=(((row + rows - 1) % rows)[None].astype(jnp.int32),),
            late=(moved,),
            flops=13 * 10**9,
        )
    with jax.named_scope("ffn_grad_rows"):
        ring_sums = []

    with jax.named_scope("d_normed2_sum"):
        branch_own, branch_other = run(
            ffn_out_kernel,
            [((amount, width), F32), ((amount, width), BF16)],
            hidden, ffn_w,
            late=(ffn_grads,),
            scratch=[pltpu.VMEM((width, units), BF16)],
        )
        d_normed_own, d_normed_other = split_sum(dn_kept, dn_arrived, ffn_grads, branch_other)

    def ring_stage(*late):
        if len(ring_sums) < rows - 1:
            moved_sum = ring_sums[-1] if ring_sums else first_grads
            step = len(ring_sums) + 2
            ring_sums.append(ring_add(ring(moved_sum), ffn_grads, step, *late))
        return ring_sums[-1]

    with jax.named_scope("ffn_grad_rows"):
        stage_one = ring_stage(d_normed_own)
    with jax.named_scope("attention_back"):
        d_residual, d_low, dq, d_gain_two, *dkv_parts = run(
            functools.partial(back_kernel, heads),
            [
                ((count, width), F32),
                ((count, width), BF16),
                ((count, q_width), BF16),
                ((8, width), F32),
            ]
            + [((count, 2 * HD), BF16)] * rows,
            d_normed_own, d_normed_other, residual, out_grad, gain_two, w_attn, cos_table,
            sin_table, queries, query_meta, key_pos, attn_out, log_sum, *kv_all,
            scalars=(core_number,),
            scratch=[pltpu.VMEM((count, width), F32), pltpu.VMEM((count, key_count), F32)],
            late=(stage_one,),
            load=True,
            vmem=60,
        )
    with jax.named_scope("out_grads"):
        out_cols = q_width // 4
        (out_parts,) = run(
            out_grad_kernel, [((4, out_cols, width), BF16)], attn_heads, d_low
        )
        out_moved = exchange(out_parts, "dp")
    with jax.named_scope("dkv_move"):
        dkv = [dkv_parts[0]] + [
            lax.ppermute(dkv_parts[step], "row", [(i + step, i) for i in range(rows - step)])
            for step in range(1, rows)
        ]
    with jax.named_scope("ffn_grad_rows"):
        stage_two = ring_stage(*dkv[1:])
    with jax.named_scope("d_lin"):
        lin_cols = lin_width // 4
        d_normed1, bias_sum, *lin_blocks = run(
            lin_back_kernel,
            [
                ((count, width), BF16),
                ((8, lin_width), F32),
                ((lin_cols, width), F32),
            ]
            + [((lin_cols, width), BF16)] * 3,
            dq, cos_table, sin_table, w_attn, normed1, *dkv,
            scalars=(target_numbers,),
            late=(stage_two, out_moved),
            scratch=[pltpu.VMEM((lin_width, width), F32)],
            load=True,
            vmem=60,
        )
    with jax.named_scope("lin_grads"):
        lin_moved = [lin_blocks[0]] + [
            dp_send(lin_blocks[step + 1], step) for step in range(3)
        ]
    with jax.named_scope("d_normed1"):
        grad_tokens, d_gain_one = run(
            final_kernel,
            [((count, width), BF16), ((8, width), F32)],
            tokens, d_normed1, swap_core(d_normed1), gain_one, d_residual,
        )
    pack_width = out_cols + lin_cols
    packet = ((EXTRA_ROWS + d_rows, pack_width), BF16)
    with jax.named_scope("ffn_grad_rows"):
        stage_three = ring_stage(*lin_moved[1:], grad_tokens)
        while len(ring_sums) < rows - 1:
            stage_three = ring_stage()
    with jax.named_scope("ffn_grad_groups"):
        flat = stage_three.reshape(3 * d_rows, units)
        ffn_done, passed = dp_gather_wide(flat)
        ffn_done = [block.reshape(3, d_rows, units) for block in ffn_done]
    with jax.named_scope("attn_grads"):
        packets = run(
            packet_kernel,
            [packet] * rows,
            d_gain_one, d_gain_two, bias_sum, out_moved, *lin_moved,
            scalars=(row_number,),
            late=(stage_three,),
            scratch=[pltpu.VMEM((width, pack_width), F32)],
        )
    with jax.named_scope("ffn_branch_sum"):
        (branch_parts,) = run(
            core_sum_kernel,
            [((4, half, width), BF16)],
            branch_own, swap_core(branch_other),
            scalars=(target_numbers,),
            late=(packets[0],),
        )
        branch_moved = exchange(branch_parts, "dp")
        (own,) = run(sum_four_kernel, [((half, width), BF16)], branch_moved)
        other = swap_core(own)
        low = jnp.where(core == 0, own, other).astype(F32)
        high = jnp.where(core == 0, other, own).astype(F32)
        output = (residual + jnp.concatenate([low, high], axis=0)).astype(BF16)
    with jax.named_scope("attn_grad_rows"):
        packets = [packets[0]] + [row_send(packets[step], step) for step in range(1, rows)]
    with jax.named_scope("attn_grad_rows"):
        (attn_sum,) = run(
            packet_sum_kernel,
            [packet],
            *packets,
            scalars=(row_number,),
            scratch=[pltpu.VMEM((rows, EXTRA_ROWS, pack_width), F32)],
        )
    with jax.named_scope("attn_grad_groups"):
        attn_done = dp_gather(attn_sum)
    with jax.named_scope("joins"):
        grad_w_gate, grad_w_up, grad_w_down_t = join(slots, ffn_done)
        grad_w_out, grad_w_query, grad_w_key, grad_w_value, smalls = run(
            functools.partial(attn_join_kernel, out_cols),
            [
                ((q_width, d_rows), F32),
                ((d_rows, q_width), F32),
                ((HD, d_rows), F32),
                ((HD, d_rows), F32),
                ((EXTRA_ROWS, pack_width), F32),
            ],
            *attn_done,
            scalars=(slots,),
            late=passed,
            scratch=[pltpu.VMEM((4, EXTRA_ROWS + d_rows, pack_width), F32)],
        )
    lines = -(-width // pack_width)
    gain_rows = [smalls[at : at + lines].reshape(-1)[:width] for at in (0, lines)]
    biases = smalls[2 * lines :].reshape(-1)[:lin_width]
    return (
        output,
        grad_tokens,
        gain_rows[0],
        grad_w_query,
        biases[:q_width],
        grad_w_key.T,
        biases[q_width:qk_width],
        grad_w_value.T,
        biases[qk_width:],
        grad_w_out,
        gain_rows[1],
        grad_w_gate,
        grad_w_up,
        grad_w_down_t.T,
    )


def solution(mesh):
    return jax.shard_map(
        functools.partial(per_device, mesh.shape["row"]),
        mesh=mesh,
        in_specs=(
            P(("dp", "row"), None),
            P(("dp", "row")),
            P(),
            P("row", "col"),
            P("col"),
            P("row", "col"),
            P("col"),
            P("row", "col"),
            P("col"),
            P("col", "row"),
            P(),
            P("row", "col"),
            P("row", "col"),
            P("col", "row"),
            P(("dp", "row"), None),
        ),
        out_specs=(
            P(("dp", "row"), None),
            P(("dp", "row"), None),
            P(),
            P("row", "col"),
            P("col"),
            P("row", "col"),
            P("col"),
            P("row", "col"),
            P("col"),
            P("col", "row"),
            P(),
            P("row", "col"),
            P("row", "col"),
            P("col", "row"),
        ),
        check_vma=False,
    )
```

```python
import functools

import jax
import jax.numpy as jnp
from jax import lax
from jax.experimental import pallas as pl
from jax.experimental.pallas import tpu as pltpu
from jax.sharding import PartitionSpec as P

HD = 64
HALF = HD // 2
NORM_EPS = 1e-06
ROPE_BASE = 1000000.0
NEG_BIG = -1e30
LANES = 128
EXTRA_ROWS = 16
BF16 = jnp.bfloat16
F32 = jnp.float32


def dot_rows(left, right):
    return lax.dot_general(left, right, (((0,), (0,)), ((), ())), preferred_element_type=F32)


def dot_cols(left, right):
    return lax.dot_general(left, right, (((1,), (1,)), ((), ())), preferred_element_type=F32)


def dot(left, right):
    return jnp.dot(left, right, preferred_element_type=F32)


def inverse_rms(values):
    return lax.rsqrt(jnp.mean(values * values, axis=1, keepdims=True) + NORM_EPS)


def norm_back(gradient, unit_rows, inv_rms, gain):
    scaled = gradient * gain
    inner = jnp.mean(scaled * unit_rows, axis=1, keepdims=True)
    return (inv_rms * (scaled - unit_rows * inner), jnp.sum(gradient * unit_rows, axis=0))


def after(value, *others):
    for other in others:
        first = other[(0,) * other.ndim].astype(F32)
        value = value + jnp.minimum(jnp.abs(first), 0.0).astype(value.dtype)
    return value


def swap_core(value):
    return lax.ppermute(value, "col", [(0, 1), (1, 0)])


def exchange(parts, axis):
    return lax.all_to_all(parts, axis, split_axis=0, concat_axis=0, tiled=True)


def gather(value, axis, size):
    return exchange(jnp.broadcast_to(value[None], (size,) + value.shape), axis)


def dp_send(value, step):
    pairs = []
    for group in range(4):
        for core in range(2):
            bits = 3 if step == 2 else 1 << ((step + core) % 2)
            pairs.append((group * 2 + core, (group ^ bits) * 2 + core))
    return lax.ppermute(value, ("dp", "col"), pairs)


def dp_gather(value):
    return [value] + [dp_send(value, step) for step in range(3)]


def dp_gather_wide(value):
    first, second = dp_send(value, 0), dp_send(value, 1)
    half = value.shape[0] // 2
    passed = (first[:half], second[half:])
    far = jnp.concatenate([dp_send(passed[0], 1), dp_send(passed[1], 0)], axis=0)
    return ([value, first, second, far], passed)


def dp_scatter_sum(parts):
    moved = [dp_send(part.astype(BF16), step) for step, part in enumerate(parts[1:])]
    return parts[0] + moved[0].astype(F32) + moved[1].astype(F32) + moved[2].astype(F32)


def pick(stacked, place):
    return lax.dynamic_index_in_dim(stacked, place, axis=0, keepdims=False)


def sum_parts(parts):
    return jnp.sum(parts.astype(F32), axis=0)


def half_turn(values):
    width = values.shape[1]
    lane = lax.broadcasted_iota(jnp.int32, values.shape, 1) % HD
    return jnp.where(
        lane < HALF, -pltpu.roll(values, width - HALF, 1), pltpu.roll(values, HALF, 1)
    )


def turned(values, cos, sin):
    copies = values.shape[1] // cos.shape[1]
    cos = jnp.concatenate([cos] * copies, axis=1)
    sin = jnp.concatenate([sin] * copies, axis=1)
    return values * cos + half_turn(values) * sin


def run(
    kernel, outs, *operands, scalars=(), late=(), far=(), scratch=(), flops=1, load=False, vmem=48
):
    leads = len(scalars) + len(late)
    first = leads + len(far)
    amount = len(operands)
    spec = pl.BlockSpec(memory_space=pltpu.VMEM)
    anywhere = pl.BlockSpec(memory_space=pl.ANY)

    def body(*refs):
        held, rest = refs[first : first + amount], refs[first + amount :]
        if load:
            sources, held, sems = held, rest[len(rest) - amount - 1 : -1], rest[-1]
            rest = rest[: len(rest) - amount - 1]
            copies = [
                pltpu.make_async_copy(source, place, sems.at[number])
                for number, (source, place) in enumerate(zip(sources, held))
            ]
            for copy in copies:
                copy.start()
            for copy in copies:
                copy.wait()
        kernel(*refs[: len(scalars)], *refs[leads:first], *held, *rest)

    places = [pltpu.VMEM(operand.shape, operand.dtype) for operand in operands] if load else []
    return pl.pallas_call(
        body,
        out_shape=tuple(jax.ShapeDtypeStruct(shape, dtype) for shape, dtype in outs),
        in_specs=[pl.BlockSpec(memory_space=pltpu.SMEM)] * len(scalars)
        + [anywhere] * (len(late) + len(far))
        + [anywhere if load else spec] * amount,
        out_specs=tuple([spec] * len(outs)),
        scratch_shapes=list(scratch)
        + places
        + ([pltpu.SemaphoreType.DMA((amount,))] if load else []),
        compiler_params=pltpu.CompilerParams(vmem_limit_bytes=vmem * 2**20),
        cost_estimate=pl.CostEstimate(flops=flops, bytes_accessed=2**20, transcendentals=0),
    )(*scalars, *late, *far, *operands)


def copy_kernel(*refs):
    out_ref = refs[-1]
    begin = 0
    for ref in refs[:-1]:
        out_ref[begin : begin + ref.shape[0], :] = ref[...]
        begin += ref.shape[0]


def stacked(blocks, *late):
    amount = sum(block.shape[0] for block in blocks)
    return run(
        copy_kernel, [((amount, blocks[0].shape[1]), blocks[0].dtype)], *blocks, late=late, vmem=32
    )[0]


def parts_kernel(*refs):
    out_ref = refs[-1]
    if len(refs) == 2:
        out_ref[...] = refs[0][...]
    else:
        for part, ref in enumerate(refs[:-1]):
            out_ref[part] = ref[...]


def place_kernel(row_ref, *refs):
    out_ref = refs[-1]
    rows = len(refs) - 1
    for step in range(rows):
        out_ref[(row_ref[0] + rows - step) % rows] = refs[step][...]


def sum_kernel(own_ref, first_ref, second_ref, both_ref, out_ref):
    summed = own_ref[...] + first_ref[...].astype(F32) + second_ref[...].astype(F32)
    out_ref[...] = (summed + both_ref[...].astype(F32)).astype(BF16)


def core_sum_kernel(target_ref, own_ref, moved_ref, out_ref):
    half = out_ref.shape[1]
    for place in range(4):
        part = slice(place * half, (place + 1) * half)
        summed = own_ref[part, :] + moved_ref[part, :].astype(F32)
        out_ref[target_ref[place]] = summed.astype(BF16)


def sum_four_kernel(parts_ref, out_ref):
    summed = parts_ref[0].astype(F32)
    for place in range(1, 4):
        summed = summed + parts_ref[place].astype(F32)
    out_ref[...] = summed.astype(BF16)


def ring_add_kernel(place_ref, parts_ref, moved_ref, out_ref, block_ref, sem):
    copy = pltpu.make_async_copy(parts_ref.at[place_ref[0]], block_ref, sem)
    copy.start()
    copy.wait()
    out_ref[...] = (moved_ref[...].astype(F32) + block_ref[...].astype(F32)).astype(BF16)


def lin_kernel(
    slot_ref, n_ref, bias_ref, cos_ref, sin_ref, seg_ref, *refs
):
    q_ref, kv_ref, w_ref = refs[4:]
    count = n_ref.shape[0]
    q_width = q_ref.shape[1]
    cols = refs[0].shape[1]
    for place in range(4):
        for slot in range(4):

            @pl.when(slot_ref[place] == slot)
            def _copy(slot=slot, place=place):
                w_ref[:, place * cols : (place + 1) * cols] = refs[slot][...]

    lin = dot(n_ref[...], w_ref[...])[:, q_width:] + bias_ref[...]
    rot = turned(lin[:, : q_width + HD], cos_ref[...], sin_ref[...])
    q_ref[...] = (rot[:, :q_width].astype(BF16).astype(F32) * HD ** (-0.5)).astype(BF16)
    kv = jnp.concatenate([rot[:, q_width:], lin[:, q_width + HD :]], axis=1)
    kv_ref[:count, :] = kv.astype(BF16)
    kv_ref[count:, :] = seg_ref[...]


def read_keys(kv_refs, meta_ref, pos_ref, bias_ref):
    count = kv_refs[0].shape[0] - EXTRA_ROWS
    joined_rows = jnp.concatenate([ref[:count, :] for ref in kv_refs], axis=0)
    docs = []
    for ref in kv_refs:
        extra = ref[count:, :].astype(F32)
        docs += [extra[line : line + 1, :] for line in range(count // LANES)]
    key_doc = jnp.concatenate(docs, axis=1)
    allowed = (pos_ref[0:1, :] <= meta_ref[:, 0:1]) & (key_doc == meta_ref[:, 1:2])
    bias_ref[...] = jnp.where(allowed, 0.0, NEG_BIG)
    return (joined_rows[:, :HD], joined_rows[:, HD:])


def attend_kernel(heads, q_ref, meta_ref, pos_ref, w_ref, *refs):
    out_ref, low_ref, lse_ref, branch_ref, bias_ref = refs[-5:]
    keys, values = read_keys(refs[:-5], meta_ref, pos_ref, bias_ref)
    lane = lax.broadcasted_iota(jnp.int32, lse_ref.shape, 1)
    lse_all = jnp.zeros(lse_ref.shape, F32)
    outs = []
    for head in range(heads):
        cols = slice(head * HD, (head + 1) * HD)
        scores = dot_cols(q_ref[:, cols], keys) + bias_ref[...]
        top = jnp.max(scores, axis=1, keepdims=True)
        weights = jnp.exp(scores - top)
        total = jnp.sum(weights, axis=1, keepdims=True)
        outs.append(dot(weights.astype(BF16), values) / total)
        lse_all = jnp.where(lane == head, top + jnp.log(total), lse_all)
    heads_sum = jnp.concatenate(outs, axis=1)
    low = heads_sum.astype(BF16)
    out_ref[...] = heads_sum
    low_ref[...] = low
    lse_ref[...] = lse_all
    branch_ref[...] = dot_cols(low, w_ref[:, : heads * HD]).astype(BF16)


def norm_kernel(core_ref, x_ref, own_ref, other_ref, gain_ref, res_ref, half_ref, norm_ref):
    half = half_ref.shape[0]
    residual = x_ref[...].astype(F32) + (own_ref[...].astype(F32) + other_ref[...].astype(F32))
    res_ref[...] = residual
    norm_ref[...] = residual * inverse_rms(residual) * gain_ref[...]
    start = pl.multiple_of(core_ref[0] * half, half)
    half_ref[...] = norm_ref[pl.ds(start, half), :].astype(BF16)


def ffn_kernel(
    n_own, n_other, g_own, g_other, w_ref,
    dn_own, dn_other, hidden_ref, dgate_ref, dup_ref, gate_ref, up_ref, down_ref,
):
    size = w_ref.shape[2]
    for place in range(w_ref.shape[0]):
        for part, ref in enumerate((gate_ref, up_ref, down_ref)):
            ref[place * size : (place + 1) * size, :] = w_ref[place, part]
    ffn_math(
        n_own, n_other, g_own, g_other, gate_ref, up_ref, down_ref,
        dn_own, dn_other, hidden_ref, dgate_ref, dup_ref,
    )


def ffn_math(
    n_own, n_other, g_own, g_other, gate_ref, up_ref, down_ref,
    dn_own, dn_other, hidden_ref, dgate_ref, dup_ref,
):
    amount = n_own.shape[0]
    tile = min(512, amount)
    for side, n_ref, g_ref in ((1, n_other, g_other), (0, n_own, g_own)):
        for begin in range(0, amount, tile):
            part = slice(begin, begin + tile)
            normed = n_ref[part, :]
            gate = dot(normed, gate_ref[...])
            up = dot(normed, up_ref[...])
            d_hidden = dot(g_ref[part, :], down_ref[...])
            sig = 1.0 / (1.0 + jnp.exp(-gate))
            silu = gate * sig
            hidden_ref[side, part, :] = (silu * up).astype(BF16)
            d_gate = (d_hidden * up * sig * (1.0 + gate * (1.0 - sig))).astype(BF16)
            d_up = (d_hidden * silu).astype(BF16)
            dgate_ref[side, part, :] = d_gate
            dup_ref[side, part, :] = d_up
            d_normed = dot_cols(d_gate, gate_ref[...]) + dot_cols(d_up, up_ref[...])
            if side == 1:
                dn_other[part, :] = d_normed.astype(BF16)
            else:
                dn_own[part, :] = d_normed


def ffn_grad_kernel(
    first_ref, n_own, n_other, g_own, g_other, dgate_ref, dup_ref, hidden_ref, out_ref, begin_ref
):
    size = out_ref.shape[2]
    item = 0
    for own, other, rights in (
        (n_own, n_other, (dgate_ref, dup_ref)),
        (g_own, g_other, (hidden_ref,)),
    ):
        own_turned, other_turned = own[...].T, other[...].T
        for right in rights:
            summed = dot(own_turned, right[0]) + dot(other_turned, right[1])
            for place in range(out_ref.shape[0]):
                block = summed[place * size : (place + 1) * size]
                out_ref[place, item] = block.astype(BF16)
            item += 1
    begin_ref[...] = out_ref[first_ref[0]]


def out_grad_kernel(heads_ref, low_ref, out_ref):
    cols = out_ref.shape[1]
    product = dot_rows(heads_ref[...], low_ref[...])
    for place in range(4):
        out_ref[place] = product[place * cols : (place + 1) * cols].astype(BF16)


def ffn_out_kernel(hidden_ref, w_ref, own_ref, other_ref, down_ref):
    size = w_ref.shape[2]
    for place in range(w_ref.shape[0]):
        down_ref[place * size : (place + 1) * size, :] = w_ref[place, 2]
    other_ref[...] = dot_cols(hidden_ref[1], down_ref[...]).astype(BF16)
    own_ref[...] = dot_cols(hidden_ref[0], down_ref[...])


def back_kernel(
    heads, core_ref, dn_own, dn_other, res_ref, grad_ref, gain_ref, w_ref, cos_ref, sin_ref,
    q_ref, meta_ref, pos_ref, out_ref, lse_ref, *refs,
):
    rows = (len(refs) - 6) // 2
    dres_ref, dlow_ref, dq_ref, dgain_ref = refs[rows : rows + 4]
    dkv_refs = refs[rows + 4 : 2 * rows + 4]
    dn_ref, bias_ref = refs[-2:]
    half = dn_own.shape[0]
    core = core_ref[0]
    dn_ref[pl.ds(pl.multiple_of(core * half, half), half), :] = dn_own[...].astype(F32)
    dn_ref[pl.ds(pl.multiple_of((1 - core) * half, half), half), :] = dn_other[...].astype(F32)
    d_normed = dn_ref[...]
    residual = res_ref[...]
    inv = inverse_rms(residual)
    unit = residual * inv
    d_norm, d_gain = norm_back(d_normed, unit, inv, gain_ref[...])
    dgain_ref[...] = jnp.broadcast_to(d_gain[None, :], dgain_ref.shape)
    d_res = grad_ref[...].astype(F32) + d_norm
    dres_ref[...] = d_res
    d_low = d_res.astype(BF16)
    dlow_ref[...] = d_low
    d_heads = dot(d_low, w_ref[:, : heads * HD]).astype(BF16)
    keys, values = read_keys(refs[:rows], meta_ref, pos_ref, bias_ref)
    d_keys = jnp.zeros(keys.shape, F32)
    d_values = jnp.zeros(keys.shape, F32)
    dqs = []
    for head in range(heads):
        cols = slice(head * HD, (head + 1) * HD)
        queries = q_ref[:, cols]
        grads = d_heads[:, cols]
        delta = jnp.sum(grads.astype(F32) * out_ref[:, cols], axis=1, keepdims=True)
        scores = dot_cols(queries, keys) + bias_ref[...]
        probs = jnp.exp(scores - lse_ref[:, head : head + 1])
        d_probs = dot_cols(grads, values)
        d_scores = (probs * (d_probs - delta)).astype(BF16)
        dqs.append(dot(d_scores, keys) * HD ** (-0.5))
        d_keys = d_keys + dot_rows(d_scores, queries)
        d_values = d_values + dot_rows(probs.astype(BF16), grads)
    dqs.append(jnp.zeros_like(dqs[0]))
    dq = turned(jnp.concatenate(dqs, axis=1), cos_ref[...], -sin_ref[...])
    dq_ref[...] = dq[:, : heads * HD].astype(BF16)
    dkv = jnp.concatenate([d_keys, d_values], axis=1).astype(BF16)
    count = dkv_refs[0].shape[0]
    for place, ref in enumerate(dkv_refs):
        ref[...] = dkv[place * count : (place + 1) * count]


def lin_back_kernel(target_ref, dq_ref, cos_ref, sin_ref, w_ref, n_ref, *refs):
    dn_ref, bias_ref = refs[-7:-5]
    blocks, product_ref = refs[-5:-1], refs[-1]
    dkv = refs[0][...].astype(F32)
    for ref in refs[1:-7]:
        dkv = dkv + ref[...].astype(F32)
    d_key = turned(dkv, cos_ref[...], -sin_ref[...])
    d_lin = jnp.concatenate(
        [dq_ref[...], d_key[:, :HD].astype(BF16), dkv[:, HD:].astype(BF16)], axis=1
    )
    product_ref[...] = dot_rows(d_lin, n_ref[...])
    cols = blocks[0].shape[0]
    for place, ref in enumerate(blocks):
        begin = pl.multiple_of(target_ref[place] * cols, cols)
        ref[...] = product_ref[pl.ds(begin, cols), :].astype(ref.dtype)
    nothing = jnp.zeros(dq_ref.shape, BF16)
    dn_ref[...] = dot_cols(jnp.concatenate([nothing, d_lin], axis=1), w_ref[...]).astype(BF16)
    bias = jnp.sum(d_lin.astype(F32), axis=0, keepdims=True)
    bias_ref[...] = jnp.broadcast_to(bias, bias_ref.shape)


def final_kernel(x_ref, own_ref, other_ref, gain_ref, dres_ref, grad_ref, dgain_ref):
    d_normed = own_ref[...].astype(F32) + other_ref[...].astype(F32)
    values = x_ref[...].astype(F32)
    inv = inverse_rms(values)
    d_norm, d_gain = norm_back(d_normed, values * inv, inv, gain_ref[...])
    grad_ref[...] = (dres_ref[...] + d_norm).astype(BF16)
    dgain_ref[...] = jnp.broadcast_to(d_gain[None, :], dgain_ref.shape)


def packet_kernel(row_ref, gain_one, gain_two, bias_ref, *refs):
    pack_ref = refs[-1]
    packets = refs[5:-1]
    out_ref = refs[0]
    out_sum = out_ref[0].astype(F32)
    for place in range(1, 4):
        out_sum = out_sum + out_ref[place].astype(F32)
    lin_sum = refs[1][...]
    for ref in refs[2:5]:
        lin_sum = lin_sum + ref[...].astype(F32)
    pack_ref[...] = jnp.concatenate([out_sum, lin_sum], axis=0).T
    cols = pack_ref.shape[1]
    lines = []
    for ref in (gain_one, gain_two, bias_ref):
        values = ref[0:1, :]
        spare = -values.shape[1] % cols
        values = jnp.concatenate([values, jnp.zeros((1, spare), F32)], axis=1)
        lines += [values[:, at : at + cols] for at in range(0, values.shape[1], cols)]
    lines.append(jnp.zeros((EXTRA_ROWS - len(lines), cols), F32))
    small = jnp.concatenate(lines, axis=0).astype(BF16)
    rows = len(packets)
    size = pack_ref.shape[0] // rows
    for step, packet in enumerate(packets):
        begin = pl.multiple_of(((row_ref[0] + step) % rows) * size, size)
        packet[:EXTRA_ROWS, :] = small
        packet[EXTRA_ROWS:, :] = pack_ref[pl.ds(begin, size), :].astype(BF16)


def packet_sum_kernel(row_ref, *refs):
    rows = len(refs) - 2
    out_ref, small_ref = refs[-2:]
    summed = refs[0][EXTRA_ROWS:, :].astype(F32)
    for ref in refs[1:rows]:
        summed = summed + ref[EXTRA_ROWS:, :].astype(F32)
    for step in range(rows):
        small_ref[(row_ref[0] + rows - step) % rows] = refs[step][:EXTRA_ROWS, :].astype(F32)
    small = small_ref[0]
    for place in range(1, rows):
        small = small + small_ref[place]
    out_ref[:EXTRA_ROWS, :] = small.astype(BF16)
    out_ref[EXTRA_ROWS:, :] = summed.astype(BF16)


def join_kernel(slot_ref, *refs):
    amount = len(refs)
    groups = 0
    while 4 * groups + sum(refs[4 * i].shape[0] for i in range(groups)) < amount:
        groups += 1
    outs = refs[4 * groups :]
    index = 0
    for number in range(groups):
        blocks = refs[4 * number : 4 * number + 4]
        cols = blocks[0].shape[2]
        for item in range(blocks[0].shape[0]):
            for place in range(4):
                for slot in range(4):

                    @pl.when(slot_ref[place] == slot)
                    def _copy(index=index, item=item, slot=slot, place=place, blocks=blocks):
                        value = blocks[slot][item].astype(F32)
                        outs[index][:, place * cols : (place + 1) * cols] = value

            index += 1


def join(slots, *groups):
    return run(
        join_kernel,
        [
            ((group[0].shape[1], 4 * group[0].shape[2]), F32)
            for group in groups
            for _ in range(group[0].shape[0])
        ],
        *[block for group in groups for block in group],
        scalars=(slots,),
        vmem=32,
    )


def attn_join_kernel(out_cols, slot_ref, *refs):
    out_ref, query_ref, key_ref, value_ref, gain_ref, part_ref = refs[4:]
    for place in range(4):
        for slot in range(4):

            @pl.when(slot_ref[place] == slot)
            def _copy(slot=slot, place=place):
                part_ref[place] = refs[slot][...].astype(F32)

    parts = [part_ref[place, EXTRA_ROWS:, :] for place in range(4)]
    out_ref[...] = jnp.concatenate([part[:, :out_cols] for part in parts], axis=1).T
    lin = jnp.concatenate([part[:, out_cols:] for part in parts], axis=1)
    q_width = query_ref.shape[1]
    query_ref[...] = lin[:, :q_width]
    key_ref[...] = lin[:, q_width : q_width + HD].T
    value_ref[...] = lin[:, q_width + HD :].T
    gains = part_ref[0, :EXTRA_ROWS, :]
    for place in range(1, 4):
        gains = gains + part_ref[place, :EXTRA_ROWS, :]
    gain_ref[...] = gains


def per_device(
    rows,
    tokens,
    segment_ids,
    attn_gain,
    w_query,
    b_query,
    w_key,
    b_key,
    w_value,
    b_value,
    w_out,
    ffn_gain,
    w_gate,
    w_up,
    w_down,
    out_grad,
):
    count, width = tokens.shape
    half = count // 2
    d_rows = w_query.shape[0]
    q_width = w_query.shape[1]
    qk_width = q_width + HD
    lin_width = qk_width + HD
    heads = q_width // HD
    units = w_gate.shape[1] // 4
    row = lax.axis_index("row")
    group = lax.axis_index("dp")
    core = lax.axis_index("col")

    targets = [group, group ^ (1 + core), group ^ (2 - core), group ^ 3]
    slots = []
    for place in range(4):
        relative = group ^ place
        flipped = (relative & 1) * 2 + (relative >> 1)
        slots.append(jnp.where(core == 0, relative, flipped))
    slots = jnp.stack(slots).astype(jnp.int32)
    target_numbers = jnp.stack(targets).astype(jnp.int32)
    core_number = core[None].astype(jnp.int32)

    def row_send(value, step):
        return lax.ppermute(value, "row", [(i, (i + step) % rows) for i in range(rows)])

    row_number = row[None].astype(jnp.int32)

    def ring(value):
        return row_send(value, 1)

    def ring_add(moved, parts, step, *late):
        place = ((row + rows - step) % rows)[None].astype(jnp.int32)
        return run(
            ring_add_kernel,
            [(moved.shape, BF16)],
            moved,
            scalars=(place,),
            late=late,
            far=(parts,),
            scratch=[pltpu.VMEM(moved.shape, BF16), pltpu.SemaphoreType.DMA],
        )[0]

    gain_one = attn_gain.astype(F32)[None, :]
    gain_two = ffn_gain.astype(F32)[None, :]
    inputs = tokens.astype(F32)
    normed1 = (inputs * inverse_rms(inputs) * gain_one).astype(BF16)
    def own_half(values):
        return lax.dynamic_slice_in_dim(values, core * half, half, axis=0)

    with jax.named_scope("out_grad_gather"):
        grad_blocks = dp_gather(own_half(out_grad))
        grad_own = stacked(grad_blocks)
        grad_other = swap_core(grad_own)
    with jax.named_scope("attn_weights"):
        block = jnp.concatenate([w_out.T, w_query, w_key, w_value], axis=1)
        block_cols = block.shape[1] // 4
        own_quarter = lax.dynamic_slice_in_dim(block, group * block_cols, block_cols, axis=1)
        quarters = gather(own_quarter, "row", rows).reshape(width, block_cols)
        w_blocks = dp_gather_wide(stacked([quarters], *grad_blocks[1:]))[0]

    def split_gather(own, *late):
        own = stacked(dp_gather(own), *late)
        return (own, swap_core(own))

    def split_send(own, other):
        moved = swap_core(other)
        blocks = moved.reshape(4, half, width)
        own = own.reshape(4, half, width)
        parts = [own[place] + blocks[place].astype(F32) for place in range(4)]
        arrived = [dp_send(part.astype(BF16), step) for step, part in enumerate(parts[1:])]
        return (parts[0], arrived, moved)

    def split_sum(own, arrived, *late):
        done = run(sum_kernel, [((half, width), BF16)], own, *arrived, late=late)[0]
        return (done, swap_core(done))

    bias = jnp.concatenate([b_query, b_key, b_value]).astype(F32)[None, :]
    positions = (row * count + jnp.arange(count, dtype=jnp.int32)).astype(F32)
    ladder = (jnp.arange(2 * HD, dtype=jnp.int32) % HALF).astype(F32) * (2.0 / HD)
    angles = positions[:, None] * jnp.exp(-ladder * jnp.log(ROPE_BASE))[None, :]
    cos_table, sin_table = jnp.cos(angles), jnp.sin(angles)
    seg_rows = count // LANES
    seg_own = segment_ids.astype(BF16).reshape(seg_rows, LANES)
    seg_own = jnp.pad(seg_own, ((0, EXTRA_ROWS - seg_rows), (0, 0)))
    query_meta = jnp.stack([positions, segment_ids.astype(F32)], axis=1)
    with jax.named_scope("ffn_weights"):
        own_ffn = [
            lax.dynamic_slice_in_dim(weight, group * units, units, axis=1)
            for weight in (w_gate, w_up, w_down.T)
        ]
        part = ((3, d_rows, units), BF16)
        (own_ffn,) = run(parts_kernel, [part], *own_ffn, late=(quarters,))
        ffn_pieces = [own_ffn, ring(own_ffn)]
    with jax.named_scope("lin"):
        queries, kv_own, w_attn = run(
            lin_kernel,
            [
                ((count, q_width), BF16),
                ((count + EXTRA_ROWS, 2 * HD), BF16),
                ((width, 4 * block_cols), BF16),
            ],
            normed1, bias, cos_table, sin_table, seg_own, *w_blocks,
            scalars=(slots,),
            load=True,
            vmem=60,
        )
    with jax.named_scope("kv_move"):
        kv_all = [kv_own] + [
            lax.ppermute(kv_own, "row", [(i, i + step) for i in range(rows - step)])
            for step in range(1, rows)
        ]
    with jax.named_scope("ffn_weights"):
        ffn_pieces.append(ring(run(parts_kernel, [part], ffn_pieces[1], late=kv_all[1:])[0]))
    block = jnp.repeat(jnp.arange(rows, dtype=jnp.int32), count)
    within = jnp.tile(jnp.arange(count, dtype=jnp.int32), rows)
    key_pos = jnp.where(block <= row, (row - block) * count + within, 2**30)
    key_pos = jnp.broadcast_to(key_pos.astype(F32)[None, :], (8, rows * count))

    key_count = rows * count
    with jax.named_scope("attention"):
        attn_out, attn_heads, log_sum, branch = run(
            functools.partial(attend_kernel, heads),
            [
                ((count, q_width), F32),
                ((count, q_width), BF16),
                ((count, LANES), F32),
                ((count, width), BF16),
            ],
            queries, query_meta, key_pos, w_attn, *kv_all,
            scratch=[pltpu.VMEM((count, key_count), F32)],
            load=True,
            vmem=60,
        )
        residual, normed2 = run(
            norm_kernel,
            [((count, width), F32), ((half, width), BF16)],
            tokens, branch, swap_core(branch), gain_two,
            scalars=(core_number,),
            late=(grad_other,),
            scratch=[pltpu.VMEM((count, width), F32)],
        )

    with jax.named_scope("ffn_weights"):
        for _ in range(3, rows):
            onward = run(parts_kernel, [part], ffn_pieces[-1], late=(normed2,))[0]
            ffn_pieces.append(ring(onward))
    with jax.named_scope("normed2_gather"):
        normed_own, normed_other = split_gather(normed2, ffn_pieces[-1])
    with jax.named_scope("ffn_weights"):
        (ffn_w,) = run(
            place_kernel,
            [((rows, 3, d_rows, units), BF16)],
            *ffn_pieces,
            scalars=(row_number,),
            vmem=32,
        )
    amount = 4 * half
    wide = ((2, amount, units), BF16)
    ffn_outs = [((amount, width), F32), ((amount, width), BF16), wide, wide, wide]
    with jax.named_scope("ffn"):
        dn_own, dn_other, hidden, d_gate, d_up = run(
            ffn_kernel,
            ffn_outs,
            normed_own, normed_other, grad_own, grad_other, ffn_w,
            scratch=[pltpu.VMEM((width, units), BF16)] * 3,
            flops=13 * 10**9,
        )
    with jax.named_scope("d_normed2_sum"):
        dn_kept, dn_arrived, moved = split_send(dn_own, dn_other)
    with jax.named_scope("ffn_grads"):
        ffn_grads, first_grads = run(
            ffn_grad_kernel,
            [((rows, 3, d_rows, units), BF16), part],
            normed_own, normed_other, grad_own, grad_other, d_gate, d_up, hidden,
            scalars=(((row + rows - 1) % rows)[None].astype(jnp.int32),),
            late=(moved,),
            flops=13 * 10**9,
        )
    with jax.named_scope("ffn_grad_rows"):
        ring_sums = []

    with jax.named_scope("d_normed2_sum"):
        branch_own, branch_other = run(
            ffn_out_kernel,
            [((amount, width), F32), ((amount, width), BF16)],
            hidden, ffn_w,
            late=(ffn_grads,),
            scratch=[pltpu.VMEM((width, units), BF16)],
        )
        d_normed_own, d_normed_other = split_sum(dn_kept, dn_arrived, ffn_grads, branch_other)

    def ring_stage(*late):
        if len(ring_sums) < rows - 1:
            moved_sum = ring_sums[-1] if ring_sums else first_grads
            step = len(ring_sums) + 2
            ring_sums.append(ring_add(ring(moved_sum), ffn_grads, step, *late))
        return ring_sums[-1]

    with jax.named_scope("ffn_grad_rows"):
        stage_one = ring_stage(d_normed_own)
    with jax.named_scope("attention_back"):
        d_residual, d_low, dq, d_gain_two, *dkv_parts = run(
            functools.partial(back_kernel, heads),
            [
                ((count, width), F32),
                ((count, width), BF16),
                ((count, q_width), BF16),
                ((8, width), F32),
            ]
            + [((count, 2 * HD), BF16)] * rows,
            d_normed_own, d_normed_other, residual, out_grad, gain_two, w_attn, cos_table,
            sin_table, queries, query_meta, key_pos, attn_out, log_sum, *kv_all,
            scalars=(core_number,),
            scratch=[pltpu.VMEM((count, width), F32), pltpu.VMEM((count, key_count), F32)],
            late=(stage_one,),
            load=True,
            vmem=60,
        )
    with jax.named_scope("out_grads"):
        out_cols = q_width // 4
        (out_parts,) = run(
            out_grad_kernel, [((4, out_cols, width), BF16)], attn_heads, d_low
        )
        out_moved = exchange(out_parts, "dp")
    with jax.named_scope("dkv_move"):
        dkv = [dkv_parts[0]] + [
            lax.ppermute(dkv_parts[step], "row", [(i + step, i) for i in range(rows - step)])
            for step in range(1, rows)
        ]
    with jax.named_scope("ffn_grad_rows"):
        stage_two = ring_stage(*dkv[1:])
    with jax.named_scope("d_lin"):
        lin_cols = lin_width // 4
        d_normed1, bias_sum, *lin_blocks = run(
            lin_back_kernel,
            [
                ((count, width), BF16),
                ((8, lin_width), F32),
                ((lin_cols, width), F32),
            ]
            + [((lin_cols, width), BF16)] * 3,
            dq, cos_table, sin_table, w_attn, normed1, *dkv,
            scalars=(target_numbers,),
            late=(stage_two, out_moved),
            scratch=[pltpu.VMEM((lin_width, width), F32)],
            load=True,
            vmem=60,
        )
    with jax.named_scope("lin_grads"):
        lin_moved = [lin_blocks[0]] + [
            dp_send(lin_blocks[step + 1], step) for step in range(3)
        ]
    with jax.named_scope("d_normed1"):
        grad_tokens, d_gain_one = run(
            final_kernel,
            [((count, width), BF16), ((8, width), F32)],
            tokens, d_normed1, swap_core(d_normed1), gain_one, d_residual,
        )
    pack_width = out_cols + lin_cols
    packet = ((EXTRA_ROWS + d_rows, pack_width), BF16)
    with jax.named_scope("ffn_grad_rows"):
        stage_three = ring_stage(*lin_moved[1:], grad_tokens)
        while len(ring_sums) < rows - 1:
            stage_three = ring_stage()
    with jax.named_scope("ffn_grad_groups"):
        flat = stage_three.reshape(3 * d_rows, units)
        ffn_done, passed = dp_gather_wide(flat)
        ffn_done = [block.reshape(3, d_rows, units) for block in ffn_done]
    with jax.named_scope("attn_grads"):
        packets = run(
            packet_kernel,
            [packet] * rows,
            d_gain_one, d_gain_two, bias_sum, out_moved, *lin_moved,
            scalars=(row_number,),
            late=(stage_three,),
            scratch=[pltpu.VMEM((width, pack_width), F32)],
        )
    with jax.named_scope("ffn_branch_sum"):
        (branch_parts,) = run(
            core_sum_kernel,
            [((4, half, width), BF16)],
            branch_own, swap_core(branch_other),
            scalars=(target_numbers,),
            late=(packets[0],),
        )
        branch_moved = exchange(branch_parts, "dp")
        (own,) = run(sum_four_kernel, [((half, width), BF16)], branch_moved)
        other = swap_core(own)
        low = jnp.where(core == 0, own, other).astype(F32)
        high = jnp.where(core == 0, other, own).astype(F32)
        output = (residual + jnp.concatenate([low, high], axis=0)).astype(BF16)
    with jax.named_scope("attn_grad_rows"):
        packets = [packets[0]] + [row_send(packets[step], step) for step in range(1, rows)]
    with jax.named_scope("attn_grad_rows"):
        (attn_sum,) = run(
            packet_sum_kernel,
            [packet],
            *packets,
            scalars=(row_number,),
            scratch=[pltpu.VMEM((rows, EXTRA_ROWS, pack_width), F32)],
        )
    with jax.named_scope("attn_grad_groups"):
        attn_done = dp_gather(attn_sum)
    with jax.named_scope("joins"):
        grad_w_gate, grad_w_up, grad_w_down_t = join(slots, ffn_done)
        grad_w_out, grad_w_query, grad_w_key, grad_w_value, smalls = run(
            functools.partial(attn_join_kernel, out_cols),
            [
                ((q_width, d_rows), F32),
                ((d_rows, q_width), F32),
                ((HD, d_rows), F32),
                ((HD, d_rows), F32),
                ((EXTRA_ROWS, pack_width), F32),
            ],
            *attn_done,
            scalars=(slots,),
            late=passed,
            scratch=[pltpu.VMEM((4, EXTRA_ROWS + d_rows, pack_width), F32)],
        )
    lines = -(-width // pack_width)
    gain_rows = [smalls[at : at + lines].reshape(-1)[:width] for at in (0, lines)]
    biases = smalls[2 * lines :].reshape(-1)[:lin_width]
    return (
        output,
        grad_tokens,
        gain_rows[0],
        grad_w_query,
        biases[:q_width],
        grad_w_key.T,
        biases[q_width:qk_width],
        grad_w_value.T,
        biases[qk_width:],
        grad_w_out,
        gain_rows[1],
        grad_w_gate,
        grad_w_up,
        grad_w_down_t.T,
    )


def solution(mesh):
    return jax.shard_map(
        functools.partial(per_device, mesh.shape["row"]),
        mesh=mesh,
        in_specs=(
            P(("dp", "row"), None),
            P(("dp", "row")),
            P(),
            P("row", "col"),
            P("col"),
            P("row", "col"),
            P("col"),
            P("row", "col"),
            P("col"),
            P("col", "row"),
            P(),
            P("row", "col"),
            P("row", "col"),
            P("col", "row"),
            P(("dp", "row"), None),
        ),
        out_specs=(
            P(("dp", "row"), None),
            P(("dp", "row"), None),
            P(),
            P("row", "col"),
            P("col"),
            P("row", "col"),
            P("col"),
            P("row", "col"),
            P("col"),
            P("col", "row"),
            P(),
            P("row", "col"),
            P("row", "col"),
            P("col", "row"),
        ),
        check_vma=False,
    )
```
